256 devices in a mesh: front: 8 (over z), row: 4 (over y), col: 8 (over x, core).
Axes of the slice: x: 4, y: 4, z: 8, core: 2. Of those that a mesh axis runs over, the one named last changes fastest.
Arguments:
- front_entries: float32 [16384, 16384], P(('front', 'row'), 'col'), as said below
- child_updates: float32 [8, 4096, 4096], P('front', ('row', 'col')), as said below
- block_offsets: int32 [8, 32], replicated, may hold values from 0 to 127, as said below
- block_counts: int32 [8], replicated, may hold values from 16 to 32, as said below
Outputs:
- trailing: float32 [16384, 16384], P(('front', 'row'), 'col')
- panel_factor: float32 [16384, 1024], P(('front', 'row'))
The draws below stay inside these ranges and needn't reach their ends.
Inputs may be any that keep to these rules, and one draw needn't show every extreme that they name: `block_offsets`: within one child all offsets differ. Block a of a child maps to a parent block i with (i // 4) % 4 == a // 8. For each child and each of its 4 groups of 8 consecutive blocks, at most 2 blocks map to parent blocks with the same i // 16, and exactly 2 for some value in every group. `block_counts`: one child has all 32 blocks live. `front_entries`: Symmetric. The leading block, rows and columns below 1024, has all eigenvalues at least 0.6 * 2 * 512, diagonal entries in 0.6 * 2 * 512 to 1.2 * 2 * 512, and off-diagonal entries of magnitude below 0.4 * 2 * 512. Entries with exactly one index below 1024 lie in -2 to 2; where neither is, off-diagonal entries lie in -1 to 1 and diagonal entries in 2 to 6. `child_updates`: each child's block is symmetric with entries of magnitude below 0.5 / 8.
All inputs are finite; a program needn't handle non-finite values.
Results may differ from the reference program's by a relative error of at most 0.0001.
Values sent between devices are 32-bit elements; how exact they have to be, the bound alone decides.
No kernel may reach another device: no remote copies, remote signals or barrier semaphores. Data moves between devices by JAX's collectives and lax.ppermute only.
A program may use at most 128 MiB of HBM per device.

```python
import jax
import jax.numpy as jnp
from jax import lax

F = 16384
S = 4096
BLOCK = 128
PANEL = 512
PANELS = 2
CHILDREN = 8
GRID_ROWS = 4
OWNED_BLOCKS = 4
ROW_BLOCKS = 8
CHILD_BLOCKS = 32


def draw_front_entries(key, part):
    key = jax.random.fold_in(key, 3)
    subkeys = jax.random.split(key, 5)
    raw_values = jax.random.uniform(subkeys[0], (F, F), jnp.float32, -1.0, 1.0)
    pivots = jax.random.uniform(subkeys[1], (F,), jnp.float32)
    leading = PANELS * PANEL
    points = jax.random.uniform(subkeys[2], (leading, 3), jnp.float32)
    spread_draw = jax.random.uniform(subkeys[3], (leading,), jnp.float32)
    boost = jax.random.uniform(subkeys[4], (leading,), jnp.float32)
    scales = 0.6 * jnp.exp(spread_draw * jnp.log(1.6 / 0.6))
    index = jnp.arange(F)
    upper = index[:, None] < index[None, :]
    symmetric = jnp.where(upper, raw_values, raw_values.T)
    in_lead = index < leading
    one_lead = in_lead[:, None] != in_lead[None, :]
    scale = jnp.where(one_lead, 2.0, 1.0).astype(jnp.float32)
    off_diagonal = symmetric * scale
    on_diagonal = 2.0 + 4.0 * pivots
    identity = index[:, None] == index[None, :]
    whole = jnp.where(identity, on_diagonal[:, None], off_diagonal).astype(jnp.float32)
    reach = 2.5 * float(leading) ** (-1.0 / 3.0)
    apart = points[:, None, :] - points[None, :, :]
    distance = jnp.sqrt(jnp.sum(apart * apart, axis=-1))
    kernel = jnp.exp(-distance / reach)
    lead_index = jnp.arange(leading)
    lead_identity = lead_index[:, None] == lead_index[None, :]
    lead_block = 0.15 * leading * scales[:, None] * scales[None, :] * kernel
    lead_block = lead_block + jnp.where(lead_identity, (leading * (0.6 + 0.2 * boost))[:, None], 0.0)
    return whole.at[:leading, :leading].set(lead_block.astype(jnp.float32)).astype(jnp.float32)


def draw_child_updates(key, part):
    key = jax.random.fold_in(key, 5)
    raw_values = jax.random.uniform(key, (CHILDREN, S, S), jnp.float32, -1.0, 1.0)
    index = jnp.arange(S)
    upper = (index[:, None] < index[None, :])[None, :, :]
    symmetric = jnp.where(upper, raw_values, jnp.swapaxes(raw_values, 1, 2))
    return (symmetric * (0.5 / CHILDREN)).astype(jnp.float32)


def draw_block_counts(key, part):
    key = jax.random.fold_in(key, 7)
    subkeys = jax.random.split(key, 2)
    counts = jax.random.randint(subkeys[0], (CHILDREN,), CHILD_BLOCKS // 2, CHILD_BLOCKS + 1)
    fullest = jax.random.randint(subkeys[1], (), 0, CHILDREN)
    return jnp.where(jnp.arange(CHILDREN) == fullest, CHILD_BLOCKS, counts).astype(jnp.int32)


def draw_block_offsets(key, part):
    key = jax.random.fold_in(key, 9)
    subkeys = jax.random.split(key, 5)
    slots_total = 2 * CHILDREN
    paired = jax.random.randint(subkeys[0], (CHILDREN, GRID_ROWS, 1), 0, CHILDREN)
    slot_ids = jnp.arange(slots_total)[None, None, :]
    scores = jax.random.randint(subkeys[1], (CHILDREN, GRID_ROWS, slots_total), 0, 1 << 20) * slots_total + slot_ids
    scores = jnp.where(slot_ids // 2 == paired, slot_ids % 2 - 2, scores)
    ordered = jnp.argsort(scores, axis=-1, stable=True)[..., :ROW_BLOCKS]
    shuffle_scores = jax.random.randint(subkeys[2], (CHILDREN, GRID_ROWS, ROW_BLOCKS), 0, 1 << 20) * ROW_BLOCKS + jnp.arange(ROW_BLOCKS)
    shuffle = jnp.argsort(shuffle_scores, axis=-1, stable=True)
    assigned = jnp.take_along_axis(ordered, shuffle, axis=-1)
    fronts = assigned // 2
    copies = assigned % 2
    first_slot = jax.random.randint(subkeys[3], (CHILDREN, GRID_ROWS, CHILDREN), 0, OWNED_BLOCKS)
    second_slot = (first_slot + jax.random.randint(subkeys[4], (CHILDREN, GRID_ROWS, CHILDREN), 1, OWNED_BLOCKS)) % OWNED_BLOCKS
    within = jnp.where(copies == 0, jnp.take_along_axis(first_slot, fronts, axis=-1), jnp.take_along_axis(second_slot, fronts, axis=-1))
    row_group = jnp.arange(GRID_ROWS)[None, :, None]
    result = (fronts * GRID_ROWS + row_group) * OWNED_BLOCKS + within
    return result.reshape(CHILDREN, CHILD_BLOCKS).astype(jnp.int32)


def setup_inputs(seed: int = 0) -> dict:
    arg_keys = jax.random.split(jax.random.key(seed), 5)
    return {
        "front_entries": draw_front_entries(jax.random.fold_in(arg_keys[4], 71), 0),
        "child_updates": draw_child_updates(jax.random.fold_in(arg_keys[4], 71), 0),
        "block_offsets": draw_block_offsets(jax.random.fold_in(arg_keys[4], 71), 0),
        "block_counts": draw_block_counts(jax.random.fold_in(arg_keys[4], 71), 0),
    }


HIGHEST = lax.Precision.HIGHEST

def reference(front_entries, child_updates, block_offsets, block_counts):
    row_numbers = jnp.arange(S, dtype=jnp.int32)
    block_of_row = (row_numbers // BLOCK).astype(jnp.int32)

    def add_child(child_no, assembled):
        offsets_here = lax.dynamic_index_in_dim(block_offsets, child_no, 0, keepdims=False)
        count_here = lax.dynamic_index_in_dim(block_counts, child_no, 0, keepdims=False)
        update_here = lax.dynamic_index_in_dim(child_updates, child_no, 0, keepdims=False)
        parent_index = (jnp.take(offsets_here, block_of_row) * BLOCK + row_numbers % BLOCK).astype(jnp.int32)
        live_rows = block_of_row < count_here
        masked_update = jnp.where(live_rows[:, None] & live_rows[None, :], update_here, jnp.zeros_like(update_here))
        return assembled.at[parent_index[:, None], parent_index[None, :]].add(masked_update)
    assembled = lax.fori_loop(0, CHILDREN, add_child, front_entries)
    positions = jnp.arange(F, dtype=jnp.int32)
    columns_list = []
    for panel_no in range(PANELS):
        panel_start = panel_no * PANEL
        trail_start = panel_start + PANEL
        diagonal = assembled[panel_start:trail_start, panel_start:trail_start]
        factor = jnp.linalg.cholesky(diagonal)
        identity = jnp.eye(PANEL, dtype=assembled.dtype)
        inverse = jax.scipy.linalg.solve_triangular(factor, identity, lower=True)
        column = jnp.dot(assembled[:, panel_start:trail_start].astype(jnp.float32), inverse.T.astype(jnp.float32), precision=HIGHEST, preferred_element_type=jnp.float32)
        retained = positions[:, None] - panel_start >= jnp.arange(PANEL, dtype=jnp.int32)[None, :]
        column = jnp.where(retained, column, jnp.zeros_like(column))
        columns_list.append(column)
        lower_part = column[trail_start:]
        product = jnp.dot(lower_part.astype(jnp.float32), lower_part.T.astype(jnp.float32), precision=HIGHEST, preferred_element_type=jnp.float32)
        assembled = assembled.at[trail_start:, trail_start:].add(-product)
    panel_factor = jnp.concatenate(columns_list, axis=1)
    retained_rows = positions >= PANELS * PANEL
    trailing = jnp.where(retained_rows[:, None] & retained_rows[None, :], assembled, jnp.zeros_like(assembled))
    return (trailing, panel_factor)
```

```python
import functools

import jax
import jax.numpy as jnp
from jax import lax
from jax.experimental import pallas as pl
from jax.experimental.pallas import tpu as pltpu
from jax.sharding import PartitionSpec as P

BLOCK = 128
LEAD = 8
LEADING = LEAD * BLOCK
HIGHEST = lax.Precision.HIGHEST
NN = (((1,), (0,)), ((), ()))
NT = (((1,), (1,)), ((), ()))
TN = (((0,), (0,)), ((), ()))
F32 = jnp.float32
SMEM = pl.BlockSpec(memory_space=pltpu.SMEM)
VMEM = pl.BlockSpec(memory_space=pltpu.VMEM)
ANY = pl.BlockSpec(memory_space=pl.ANY)


def mm(a, b, dims):
    return lax.dot_general(a, b, dims, precision=HIGHEST, preferred_element_type=F32)


def split(x):
    high = x.astype(jnp.bfloat16)
    low = (x - high.astype(F32)).astype(jnp.bfloat16)
    return high, low


def mm3(a, b, dims):
    ah, al = a
    bh, bl = b
    dot = functools.partial(lax.dot_general, dimension_numbers=dims, preferred_element_type=F32)
    return dot(ah, bh) + (dot(al, bh) + dot(ah, bl))


def call(body, name, out_shape, in_specs, out_specs, scratch=(), flops=0, moved=0, **more):
    return pl.pallas_call(
        body,
        name=name,
        out_shape=out_shape,
        in_specs=in_specs,
        out_specs=out_specs,
        scratch_shapes=list(scratch),
        compiler_params=pltpu.CompilerParams(vmem_limit_bytes=48 << 20),
        cost_estimate=pl.CostEstimate(flops=flops, bytes_accessed=moved, transcendentals=0),
        **more,
    )


def shape(*dims):
    return jax.ShapeDtypeStruct(dims, F32)


def lead_columns_body(off, cnt, child, out):
    g = lax.axis_index("front")
    own = lax.axis_index("row") * lax.axis_size("col") + lax.axis_index("col")
    out[...] = jnp.zeros_like(out)
    live = cnt[g]
    for b in range(off.shape[1]):
        o = off[g, b]

        @pl.when((o < LEAD) & (b < live) & (own < live))
        def _():
            out[o] = child[0, :, b * BLOCK : (b + 1) * BLOCK]


def lead_rows_body(per_front, off, cnt, got, corner, panel):
    g = lax.axis_index("front")
    r = lax.axis_index("row")
    rows = got.shape[0]
    corner[...] = jnp.zeros_like(corner)
    panel[...] = jnp.zeros_like(panel)
    for j in range(rows):
        o = off[g, r * rows + j]
        f = o // per_front
        rank = jnp.int32(0)
        for i in range(j):
            rank += (off[g, r * rows + i] // per_front == f).astype(jnp.int32)

        panel[f, rank] = got[j]

        @pl.when(o < LEAD)
        def _():
            for q in range(corner.shape[0]):
                corner[q, rank] = got[j]


def gather_rows_body(per_front, to_front, off, cnt, got, base, out):
    r = lax.axis_index("row")
    f = 0 if to_front else lax.axis_index("front")
    children = got.shape[0]
    rows = off.shape[1] // lax.axis_size("row")
    owned = out.shape[0] // BLOCK
    out[...] = base[...]

    def child(g, carry):
        rank = jnp.int32(0)
        for j in range(rows):
            a = r * rows + j
            o = off[g, a]
            hit = o // per_front == f

            @pl.when(hit & (a < cnt[g]))
            def _():
                at = pl.multiple_of((o % owned) * BLOCK, BLOCK)
                out[pl.ds(at, BLOCK), :] += got[g, rank]

            rank += hit.astype(jnp.int32)
        return carry

    lax.fori_loop(0, children, child, 0)


def far_columns_body(per_col, off, cnt, child, out, sems, slots):
    g = lax.axis_index("front")
    groups = out.shape[0]
    blocks = off.shape[1]
    for c in range(groups):
        slots[c] = 0
    copies = []
    for b in range(blocks):
        o = off[g, b]
        c = o // per_col
        use = (o >= LEAD) & (b < cnt[g])
        k = jnp.minimum(slots[c], out.shape[1] - 1)
        copy = pltpu.make_async_copy(
            child.at[0, :, pl.ds(b * BLOCK, BLOCK)], out.at[c, k], sems.at[b]
        )
        copies.append((use, copy))

        @pl.when(use)
        def _():
            copy.start()
            slots[c] = k + 1

    for use, copy in copies:

        @pl.when(use)
        def _():
            copy.wait()


def far_rows_body(per_front, off, cnt, got, out, sems):
    g = lax.axis_index("front")
    r = lax.axis_index("row")
    rows = got.shape[0]
    copies = []
    for j in range(rows):
        a = r * rows + j
        o = off[g, a]
        f = o // per_front
        rank = jnp.int32(0)
        for i in range(j):
            rank += (off[g, r * rows + i] // per_front == f).astype(jnp.int32)
        use = (o >= LEAD) & (a < cnt[g])
        copy = pltpu.make_async_copy(got.at[j], out.at[f, jnp.minimum(rank, 1)], sems.at[j])
        copies.append((use, copy))

        @pl.when(use)
        def _():
            copy.start()

    for use, copy in copies:

        @pl.when(use)
        def _():
            copy.wait()


def factor_block(w):
    sub = lax.broadcasted_iota(jnp.int32, (8, BLOCK), 0)
    for lo in range(0, BLOCK, 8):
        r0 = w[lo : lo + 8, 0:BLOCK]
        r1 = w[lo : lo + 8, BLOCK : 2 * BLOCK]
        e = [jnp.broadcast_to(r0[:, lo + k : lo + k + 1], (8, BLOCK)) for k in range(8)]
        recip, across, top0, top1 = [], {}, [], []
        pivots = jnp.ones((8, BLOCK), F32)
        for i in range(8):
            row = {k: jnp.broadcast_to(e[k][i : i + 1, :], (8, BLOCK)) for k in range(i, 8)}
            inv = 1.0 / row[i]
            recip.append(inv)
            m = jnp.where(sub > i, e[i] * inv, 0.0)
            b0 = jnp.broadcast_to(r0[i : i + 1, :], (8, BLOCK))
            b1 = jnp.broadcast_to(r1[i : i + 1, :], (8, BLOCK))
            top0.append(b0)
            top1.append(b1)
            for k in range(i + 1, 8):
                across[i, k] = row[k]
                e[k] = e[k] - m * row[k]
            r0 = r0 - m * b0
            r1 = r1 - m * b1
            pivots = jnp.where(sub == i, row[i], pivots)
        scale = lax.rsqrt(pivots)
        w[lo : lo + 8, 0:BLOCK] = r0 * scale
        w[lo : lo + 8, BLOCK : 2 * BLOCK] = r1 * scale
        q = lo + 8
        while q < BLOCK:
            n = min(32, BLOCK - q)

            def tall(x):
                return jnp.concatenate([x] * (n // 8), axis=0) if n > 8 else x

            g0 = w[q : q + n, 0:BLOCK]
            g1 = w[q : q + n, BLOCK : 2 * BLOCK]
            e = [jnp.broadcast_to(g0[:, lo + k : lo + k + 1], (n, BLOCK)) for k in range(8)]
            for i in range(8):
                m = e[i] * tall(recip[i])
                for k in range(i + 1, 8):
                    e[k] = e[k] - m * tall(across[i, k])
                g0 = g0 - m * tall(top0[i])
                g1 = g1 - m * tall(top1[i])
            w[q : q + n, 0:BLOCK] = g0
            w[q : q + n, BLOCK : 2 * BLOCK] = g1
            q += n


def factor_body(a, u_ref, inv_ref, s, w):
    nb = a.shape[0]
    for c in range(nb):
        s[:, c * BLOCK : (c + 1) * BLOCK] = a[c]
    ri = lax.broadcasted_iota(jnp.int32, (BLOCK, BLOCK), 0)
    ci = lax.broadcasted_iota(jnp.int32, (BLOCK, BLOCK), 1)
    eye = (ri == ci).astype(F32)

    def step(k, carry):
        at = pl.ds(pl.multiple_of(k * BLOCK, BLOCK), BLOCK)
        w[:, 0:BLOCK] = s[at, at]
        w[:, BLOCK : 2 * BLOCK] = eye
        factor_block(w)
        inverse = jnp.where(ri >= ci, w[:, BLOCK : 2 * BLOCK], 0.0)
        inv_ref[at, :] = inverse
        u_ref[at, at] = jnp.where(ri <= ci, w[:, 0:BLOCK], 0.0)
        for kk in range(nb - 1):

            @pl.when(k == kk)
            def _():
                h = (kk + 1) * BLOCK
                u = mm(inverse, s[kk * BLOCK : h, h:], NN)
                u_ref[kk * BLOCK : h, h:] = u
                for i in range(kk + 1, nb):
                    o = (i - kk - 1) * BLOCK
                    s[i * BLOCK : (i + 1) * BLOCK, i * BLOCK :] -= mm(
                        u[:, o : o + BLOCK], u[:, o:], TN
                    )

        return carry

    lax.fori_loop(0, nb, step, 0)


def solve_body(u, inv, a, m_ref, t_ref, work):
    nb = a.shape[0]
    rows = a.shape[1]
    for c in range(nb):
        work[:, c * BLOCK : (c + 1) * BLOCK] = a[c]
    first = (lax.axis_index("front") * lax.axis_size("row") + lax.axis_index("row")) * rows
    ri = first + lax.broadcasted_iota(jnp.int32, (rows, BLOCK), 0)
    ci = lax.broadcasted_iota(jnp.int32, (rows, BLOCK), 1)
    for k in range(nb):
        at = slice(k * BLOCK, (k + 1) * BLOCK)
        m = mm(work[:, at], inv[at, :], NT)
        work[:, at] = m
        m_ref[:, at] = jnp.where(ri >= ci + k * BLOCK, m, 0.0)
        if k + 1 < nb:
            work[:, (k + 1) * BLOCK :] -= mm(m, u[at, (k + 1) * BLOCK :], NN)
    for k in reversed(range(nb)):
        at = slice(k * BLOCK, (k + 1) * BLOCK)
        x = work[:, at]
        if k + 1 < nb:
            x = x - mm(t_ref[:, (k + 1) * BLOCK :], u[at, (k + 1) * BLOCK :], NT)
        t_ref[:, at] = mm(x, inv[at, :], NN)


def final_body(per_front, per_col, off, cnt, t, pair, got, base, out):
    step = pl.program_id(0)
    f = lax.axis_index("front")
    r = lax.axis_index("row")
    c = lax.axis_index("col")
    rows = off.shape[1] // lax.axis_size("row")
    owned = out.shape[0] // BLOCK
    span = out.shape[1] // BLOCK
    width = 2 * BLOCK

    @pl.when(step == 0)
    def _():
        out[...] = base[...]

    for half in range(2):
        g = 2 * step + half
        rank = jnp.int32(0)
        for j in range(rows):
            a = r * rows + j
            o = off[g, a]
            hit = o // per_front == f
            at = pl.multiple_of((o % owned) * BLOCK, BLOCK)
            here = rank

            @pl.when(hit & (a < cnt[g]) & (o >= LEAD))
            def _():
                def column(b, k):
                    p = off[g, b]
                    use = (p // per_col == c) & (p >= LEAD) & (b < cnt[g])

                    @pl.when(use)
                    def _():
                        to = pl.multiple_of((p % span) * BLOCK, BLOCK)
                        out[pl.ds(at, BLOCK), pl.ds(to, BLOCK)] += got[half, here, k]

                    return k + use.astype(jnp.int32)

                lax.fori_loop(0, off.shape[1], column, jnp.int32(0))

            rank += hit.astype(jnp.int32)

    tt = split(t[:, pl.ds(pl.multiple_of(step * width, width), width)])
    chunk = 512
    for q in range(0, out.shape[1], chunk):
        other = jnp.concatenate([pair[0, q : q + chunk, :], pair[1, q : q + chunk, :]], axis=1)
        out[:, q : q + chunk] -= mm3(tt, split(other), NT)

    @pl.when(step == pl.num_programs(0) - 1)
    def _():
        top = f * lax.axis_size("row") + r

        @pl.when(top * out.shape[0] < LEADING)
        def _():
            out[...] = jnp.zeros_like(out)

        @pl.when(c * out.shape[1] < LEADING)
        def _():
            out[:, :LEADING] = jnp.zeros((out.shape[0], LEADING), F32)


def on_device(front_entries, child_updates, off, cnt):
    fronts = lax.axis_size("front")
    rows = lax.axis_size("row")
    cols = lax.axis_size("col")
    own_rows, own_cols = front_entries.shape
    owned = own_rows // BLOCK
    per_front = owned * rows
    per_col = own_cols // BLOCK
    r = lax.axis_index("row")
    c = lax.axis_index("col")
    row_blocks = off.shape[1] // rows
    block = (BLOCK, BLOCK)

    lead = call(
        lead_columns_body, "lead_columns", shape(cols, *block), [SMEM, SMEM, VMEM], VMEM
    )(off, cnt, child_updates)
    lead = lax.all_to_all(lead, "col", split_axis=0, concat_axis=0, tiled=True)
    strips = [front_entries[:, k * BLOCK : (k + 1) * BLOCK] for k in range(LEAD)]
    strip = jnp.where(c == 0, strips[0], 0.0)
    for k in range(1, cols):
        strip = strip + lax.ppermute(strips[k], "col", [(0, k)])
    top = jnp.where(lax.axis_index("front") == 0, strip, 0.0)
    for k in range(1, fronts):
        top = top + lax.ppermute(strip, "front", [(0, k)])
    corner, panel = call(
        functools.partial(lead_rows_body, per_front),
        "lead_rows",
        (shape(fronts, 2, *block), shape(fronts, 2, *block)),
        [SMEM, SMEM, VMEM],
        (VMEM, VMEM),
    )(off, cnt, lead)

    corner = lax.all_to_all(corner, "front", split_axis=0, concat_axis=0, tiled=True)
    piece = call(
        functools.partial(gather_rows_body, per_front, True),
        "corner_piece",
        shape(own_rows, BLOCK),
        [SMEM, SMEM, VMEM, VMEM],
        VMEM,
    )(off, cnt, corner, top)
    near = lax.ppermute(piece, "row", [(0, 1), (1, 0)])
    side = lax.ppermute(piece, "row", [(0, 3), (1, 2)])
    far = lax.ppermute(piece, "row", [(0, 2), (1, 3)])
    upper = jnp.where(r == 0, piece, jnp.where(r == 1, near, jnp.where(r == 2, far, side)))
    lower = jnp.where(r == 1, piece, jnp.where(r == 0, near, jnp.where(r == 2, side, far)))
    corner = lax.all_gather(jnp.concatenate([upper, lower], axis=0), "col", axis=0)
    u, inv = call(
        factor_body,
        "factor",
        (shape(LEADING, LEADING), shape(LEADING, BLOCK)),
        [VMEM],
        (VMEM, VMEM),
        [pltpu.VMEM((LEADING, LEADING), F32), pltpu.VMEM((BLOCK, 2 * BLOCK), F32)],
        flops=40 * 1150 * 10**6,
    )(corner)

    panel = lax.all_to_all(panel, "front", split_axis=0, concat_axis=0, tiled=True)
    strip = call(
        functools.partial(gather_rows_body, per_front, False),
        "panel_piece",
        shape(own_rows, BLOCK),
        [SMEM, SMEM, VMEM, VMEM],
        VMEM,
    )(off, cnt, panel, strip)
    mine = lax.all_gather(strip, "col", axis=0)
    swap = [
        ((i * rows + j) * cols + k, (k * rows + j) * cols + i)
        for i in range(fronts)
        for j in range(rows)
        for k in range(cols)
    ]
    across = lax.ppermute(strip, ("front", "row", "col"), swap)
    across = lax.all_gather(across, ("front", "row"), axis=0)
    across = across.reshape(LEAD, own_cols, BLOCK)
    m, t = call(
        solve_body,
        "solve",
        (shape(own_rows, LEADING), shape(own_rows, LEADING)),
        [VMEM, VMEM, VMEM],
        (VMEM, VMEM),
        [pltpu.VMEM((own_rows, LEADING), F32)],
        flops=12 * 1150 * 10**6,
    )(u, inv, mine)

    slots = 2 * rows
    rest = call(
        functools.partial(far_columns_body, per_col),
        "far_columns",
        shape(cols, slots, *block),
        [SMEM, SMEM, ANY],
        ANY,
        [pltpu.SemaphoreType.DMA((off.shape[1],)), pltpu.SMEM((cols,), jnp.int32)],
        moved=4 << 20,
    )(off, cnt, child_updates)
    rest = lax.all_to_all(rest, "col", split_axis=0, concat_axis=0, tiled=True)
    rest = call(
        functools.partial(far_rows_body, per_front),
        "far_rows",
        shape(fronts, 2, slots, *block),
        [SMEM, SMEM, ANY],
        ANY,
        [pltpu.SemaphoreType.DMA((row_blocks,))],
        moved=8 << 20,
    )(off, cnt, rest)
    rest = lax.all_to_all(rest, "front", split_axis=0, concat_axis=0, tiled=True)
    trailing = pl.pallas_call(
        functools.partial(final_body, per_front, per_col),
        name="final",
        grid=(LEAD // 2,),
        out_shape=shape(own_rows, own_cols),
        in_specs=[
            SMEM,
            SMEM,
            pl.BlockSpec((own_rows, LEADING), lambda i: (0, 0)),
            pl.BlockSpec((2, own_cols, BLOCK), lambda i: (i, 0, 0)),
            pl.BlockSpec((2, 2, slots, *block), lambda i: (i, 0, 0, 0, 0)),
            pl.BlockSpec((own_rows, own_cols), lambda i: (0, 0)),
        ],
        out_specs=pl.BlockSpec((own_rows, own_cols), lambda i: (0, 0)),
        compiler_params=pltpu.CompilerParams(vmem_limit_bytes=56 << 20),
        cost_estimate=pl.CostEstimate(
            flops=12 * 1150 * 10**6, bytes_accessed=24 << 20, transcendentals=0
        ),
    )(off, cnt, t, across, rest, front_entries)
    return trailing, m


def solution(mesh):
    placed = (P(("front", "row"), "col"), P("front", ("row", "col"), None), P(), P())
    return jax.shard_map(
        on_device,
        mesh=mesh,
        in_specs=placed,
        out_specs=(P(("front", "row"), "col"), P(("front", "row"), None)),
        check_vma=False,
    )
```

```python
import functools

import jax
import jax.numpy as jnp
from jax import lax
from jax.experimental import pallas as pl
from jax.experimental.pallas import tpu as pltpu
from jax.sharding import PartitionSpec as P

BLOCK = 128
LEAD = 8
LEADING = LEAD * BLOCK
SLOTS = 4
HIGHEST = lax.Precision.HIGHEST
NN = (((1,), (0,)), ((), ()))
NT = (((1,), (1,)), ((), ()))
TN = (((0,), (0,)), ((), ()))
F32 = jnp.float32
SMEM = pl.BlockSpec(memory_space=pltpu.SMEM)
VMEM = pl.BlockSpec(memory_space=pltpu.VMEM)
ANY = pl.BlockSpec(memory_space=pl.ANY)


def mm(a, b, dims):
    return lax.dot_general(a, b, dims, precision=HIGHEST, preferred_element_type=F32)


def split(x):
    high = x.astype(jnp.bfloat16)
    low = (x - high.astype(F32)).astype(jnp.bfloat16)
    return high, low


def mm3(a, b, dims):
    ah, al = a
    bh, bl = b
    dot = functools.partial(lax.dot_general, dimension_numbers=dims, preferred_element_type=F32)
    return dot(ah, bh) + (dot(al, bh) + dot(ah, bl))


def call(body, name, out_shape, in_specs, out_specs, scratch=(), flops=0, moved=0, **more):
    return pl.pallas_call(
        body,
        name=name,
        out_shape=out_shape,
        in_specs=in_specs,
        out_specs=out_specs,
        scratch_shapes=list(scratch),
        compiler_params=pltpu.CompilerParams(vmem_limit_bytes=48 << 20),
        cost_estimate=pl.CostEstimate(flops=flops, bytes_accessed=moved, transcendentals=0),
        **more,
    )


def shape(*dims):
    return jax.ShapeDtypeStruct(dims, F32)


def lead_columns_body(off, cnt, child, out):
    g = lax.axis_index("front")
    own = lax.axis_index("row") * lax.axis_size("col") + lax.axis_index("col")
    out[...] = jnp.zeros_like(out)
    live = cnt[g]
    for b in range(off.shape[1]):
        o = off[g, b]

        @pl.when((o < LEAD) & (b < live) & (own < live))
        def _():
            out[o] = child[0, :, b * BLOCK : (b + 1) * BLOCK]


def lead_rows_body(per_front, off, cnt, got, part, out):
    g = lax.axis_index("front")
    r = lax.axis_index("row")
    rows = got.shape[0]
    out[...] = jnp.zeros_like(out)
    for q in range(out.shape[0]):
        out[q, 4 * BLOCK :] = part[...]
    for j in range(rows):
        o = off[g, r * rows + j]
        f = o // per_front
        rank = jnp.int32(0)
        for i in range(j):
            rank += (off[g, r * rows + i] // per_front == f).astype(jnp.int32)

        out[f, pl.ds(pl.multiple_of((2 + rank) * BLOCK, BLOCK), BLOCK)] = got[j]

        @pl.when(o < LEAD)
        def _():
            for q in range(out.shape[0]):
                out[q, pl.ds(pl.multiple_of(rank * BLOCK, BLOCK), BLOCK)] = got[j]


def pieces_body(per_front, off, cnt, got, base, _, corner, panel):
    r = lax.axis_index("row")
    own = lax.axis_index("front")
    children = got.shape[0]
    rows = off.shape[1] // lax.axis_size("row")
    owned = panel.shape[0] // BLOCK
    part = corner.shape[0] // children
    panel[...] = base[...]
    for g in range(children):
        corner[g * part : (g + 1) * part] = got[g, 4 * BLOCK :]

    def child(g, carry):
        ranks = [jnp.int32(0), jnp.int32(0)]
        for j in range(rows):
            a = r * rows + j
            o = off[g, a]
            at = pl.ds(pl.multiple_of((o % owned) * BLOCK, BLOCK), BLOCK)
            for i, (f, out) in enumerate(((0, corner), (own, panel))):
                hit = o // per_front == f
                here = pl.ds(pl.multiple_of((2 * i + ranks[i]) * BLOCK, BLOCK), BLOCK)

                @pl.when(hit & (a < cnt[g]))
                def _():
                    out[at, :] += got[g, here]

                ranks[i] += hit.astype(jnp.int32)
        return carry

    lax.fori_loop(0, children, child, 0)


def plan_body(per_col, lanes, off, cnt, _, place, holder, items, pair, sizes, taken, pairs):
    children, blocks = off.shape
    for i in range(lanes * lanes):
        pairs[i] = 0
    sizes[0] = 0
    sizes[1] = 0

    def child(g, carry):
        for m in range(lanes):
            taken[m] = 0
        for b in range(blocks):
            holder[g, b] = -1
        first = sizes[0]

        def own_lane(b, n):
            o = off[g, b]
            c = o // per_col
            k = taken[c]
            use = (o >= LEAD) & (b < cnt[g])
            fits = use & (k < SLOTS)
            place[g, b] = jnp.where(fits, c * SLOTS + k, -1)

            @pl.when(fits)
            def _():
                holder[g, c * SLOTS + k] = b
                taken[c] = k + 1

            spill = use & (k >= SLOTS)

            @pl.when(spill)
            def _():
                items[n] = g * blocks + b

            return n + spill.astype(jnp.int32)

        last = lax.fori_loop(0, blocks, own_lane, first)
        sizes[0] = last

        def other_lane(n, carry):
            b = items[n] % blocks
            c = off[g, b] // per_col
            best = jnp.int32(1 << 20)
            lane = jnp.int32(0)
            for m in range(lanes):
                score = jnp.where(taken[m] < SLOTS, pairs[m * lanes + c], 1 << 20)
                lane = jnp.where(score < best, m, lane)
                best = jnp.minimum(score, best)
            place[g, b] = lane * SLOTS + taken[lane]
            pair[n] = best
            taken[lane] += 1
            pairs[lane * lanes + c] = best + 1
            sizes[1] = jnp.maximum(sizes[1], best + 1)
            return carry

        lax.fori_loop(first, last, other_lane, 0)
        return carry

    lax.fori_loop(0, children, child, 0)


def far_columns_body(place, child, out, sems):
    g = lax.axis_index("front")
    c = lax.axis_index("col")
    lanes = out.shape[0]
    copies = []
    for b in range(place.shape[1]):
        p = place[g, b]
        to = jnp.maximum(p, 0)
        copy = pltpu.make_async_copy(
            child.at[0, :, pl.ds(b * BLOCK, BLOCK)],
            out.at[(to // SLOTS + lanes - c) % lanes, to % SLOTS],
            sems.at[b],
        )
        copies.append((p >= 0, copy))

        @pl.when(p >= 0)
        def _():
            copy.start()

    for use, copy in copies:

        @pl.when(use)
        def _():
            copy.wait()


def far_rows_body(per_front, off, cnt, *refs):
    *got, out, sems = refs
    g = lax.axis_index("front")
    r = lax.axis_index("row")
    c = lax.axis_index("col")
    rows = len(got)
    copies = []
    for away in range(rows):
        j = (c + rows - away) % rows
        a = r * rows + j
        o = off[g, a]
        f = o // per_front
        rank = jnp.int32(0)
        for i in range(rows):
            rank += ((off[g, r * rows + i] // per_front == f) & (i < j)).astype(jnp.int32)
        use = (o >= LEAD) & (a < cnt[g])
        copy = pltpu.make_async_copy(
            got[away].at[0], out.at[f, jnp.minimum(rank, 1)], sems.at[away]
        )
        copies.append((use, copy))

        @pl.when(use)
        def _():
            copy.start()

    for use, copy in copies:

        @pl.when(use)
        def _():
            copy.wait()


def spill_body(per_col, turn, off, place, items, pair, sizes, got, _, out):
    c = lax.axis_index("col")
    out[...] = jnp.zeros_like(out)
    blocks = off.shape[1]

    def item(n, carry):
        g = items[n] // blocks
        b = items[n] % blocks
        p = place[g, b]

        @pl.when((pair[n] == turn[0]) & (p // SLOTS == c))
        def _():
            out[off[g, b] // per_col] = got[g, :, p % SLOTS]

        return carry

    lax.fori_loop(0, sizes[0], item, 0)


def each_row(per_front, g, off, cnt, add):
    f = lax.axis_index("front")
    r = lax.axis_index("row")
    rows = off.shape[1] // lax.axis_size("row")
    owned = per_front // lax.axis_size("row")
    rank = jnp.int32(0)
    for j in range(rows):
        a = r * rows + j
        o = off[g, a]
        hit = o // per_front == f
        row = pl.ds(pl.multiple_of((o % owned) * BLOCK, BLOCK), BLOCK)
        here = rank

        @pl.when(hit & (a < cnt[g]) & (o >= LEAD))
        def _():
            add(row, here)

        rank += hit.astype(jnp.int32)


def own_column(per_col, p):
    return pl.ds(pl.multiple_of((p % per_col) * BLOCK, BLOCK), BLOCK)


def spill_add(per_front, per_col, turn, off, cnt, place, items, pair, sizes, spilt, out):
    c = lax.axis_index("col")
    blocks = off.shape[1]

    def item(n, carry):
        g = items[n] // blocks
        b = items[n] % blocks
        p = off[g, b]
        lane = jnp.maximum(place[g, b], 0) // SLOTS

        @pl.when((pair[n] == turn) & (p // per_col == c))
        def _():
            def add(row, rank):
                out[row, own_column(per_col, p)] += spilt[lane, rank]

            each_row(per_front, g, off, cnt, add)

        return carry

    lax.fori_loop(0, sizes[0], item, 0)


def spill_add_body(per_front, per_col, turn, off, cnt, place, items, pair, sizes, spilt, base, out):
    out[...] = base[...]
    spill_add(per_front, per_col, turn[0], off, cnt, place, items, pair, sizes, spilt, out)


def assemble_body(per_front, per_col, off, cnt, holder, got, base, out):
    c = lax.axis_index("col")
    step = pl.program_id(0)

    @pl.when(step == 0)
    def _():
        out[...] = base[...]

    for half in range(got.shape[0]):
        g = got.shape[0] * step + half

        def add(row, rank):
            for k in range(SLOTS):
                b = holder[g, c * SLOTS + k]

                @pl.when(b >= 0)
                def _():
                    at = own_column(per_col, off[g, jnp.maximum(b, 0)])
                    out[row, at] += got[half, rank, k]

        each_row(per_front, g, off, cnt, add)


def factor_block(w):
    sub = lax.broadcasted_iota(jnp.int32, (8, BLOCK), 0)
    for lo in range(0, BLOCK, 8):
        r0 = w[lo : lo + 8, 0:BLOCK]
        r1 = w[lo : lo + 8, BLOCK : 2 * BLOCK]
        e = [jnp.broadcast_to(r0[:, lo + k : lo + k + 1], (8, BLOCK)) for k in range(8)]
        recip, across, top0, top1 = [], {}, [], []
        pivots = jnp.ones((8, BLOCK), F32)
        for i in range(8):
            row = {k: jnp.broadcast_to(e[k][i : i + 1, :], (8, BLOCK)) for k in range(i, 8)}
            inv = 1.0 / row[i]
            recip.append(inv)
            m = jnp.where(sub > i, e[i] * inv, 0.0)
            b0 = jnp.broadcast_to(r0[i : i + 1, :], (8, BLOCK))
            b1 = jnp.broadcast_to(r1[i : i + 1, :], (8, BLOCK))
            top0.append(b0)
            top1.append(b1)
            for k in range(i + 1, 8):
                across[i, k] = row[k]
                e[k] = e[k] - m * row[k]
            r0 = r0 - m * b0
            r1 = r1 - m * b1
            pivots = jnp.where(sub == i, row[i], pivots)
        scale = lax.rsqrt(pivots)
        w[lo : lo + 8, 0:BLOCK] = r0 * scale
        w[lo : lo + 8, BLOCK : 2 * BLOCK] = r1 * scale
        q = lo + 8
        while q < BLOCK:
            n = min(32, BLOCK - q)

            def tall(x):
                return jnp.concatenate([x] * (n // 8), axis=0) if n > 8 else x

            g0 = w[q : q + n, 0:BLOCK]
            g1 = w[q : q + n, BLOCK : 2 * BLOCK]
            e = [jnp.broadcast_to(g0[:, lo + k : lo + k + 1], (n, BLOCK)) for k in range(8)]
            for i in range(8):
                m = e[i] * tall(recip[i])
                for k in range(i + 1, 8):
                    e[k] = e[k] - m * tall(across[i, k])
                g0 = g0 - m * tall(top0[i])
                g1 = g1 - m * tall(top1[i])
            w[q : q + n, 0:BLOCK] = g0
            w[q : q + n, BLOCK : 2 * BLOCK] = g1
            q += n


def factor_body(start, blocks, fresh, a, _, s, inv_ref, w):
    ri = lax.broadcasted_iota(jnp.int32, (BLOCK, BLOCK), 0)
    ci = lax.broadcasted_iota(jnp.int32, (BLOCK, BLOCK), 1)
    eye = (ri == ci).astype(F32)
    if fresh:
        for c in range(LEAD):
            s[:, c * BLOCK : (c + 1) * BLOCK] = a[c]
    else:
        s[...] = a[...]

    def step(k, carry):
        at = pl.ds(pl.multiple_of(k * BLOCK, BLOCK), BLOCK)
        w[:, 0:BLOCK] = s[at, at]
        w[:, BLOCK : 2 * BLOCK] = eye
        factor_block(w)
        inverse = jnp.where(ri >= ci, w[:, BLOCK : 2 * BLOCK], 0.0)
        inv_ref[pl.ds(pl.multiple_of((k - start) * BLOCK, BLOCK), BLOCK), :] = inverse
        for kk in range(start, min(start + blocks, LEAD - 1)):

            @pl.when(k == kk)
            def _():
                h = (kk + 1) * BLOCK
                u = mm(inverse, s[kk * BLOCK : h, h:], NN)
                s[kk * BLOCK : h, h:] = u
                for i in range(kk + 1, LEAD):
                    o = (i - kk - 1) * BLOCK
                    s[i * BLOCK : (i + 1) * BLOCK, i * BLOCK :] -= mm(
                        u[:, o : o + BLOCK], u[:, o:], TN
                    )

        return carry

    lax.fori_loop(start, start + blocks, step, 0)


def factor(start, blocks, fresh, a, after):
    return call(
        functools.partial(factor_body, start, blocks, fresh),
        "factor",
        (shape(LEADING, LEADING), shape(blocks * BLOCK, BLOCK)),
        [VMEM, ANY],
        (VMEM, VMEM),
        [pltpu.VMEM((BLOCK, 2 * BLOCK), F32)],
        flops=20 * 1150 * 10**6,
    )(a, after)


def solve_body(u, inv_low, inv_high, *refs):
    *a, m_ref, t_ref, work = refs
    nb = len(a)
    rows = a[0].shape[0]
    half = nb // 2
    lane = lax.axis_index("col")
    wide = 2 * BLOCK

    def inverse(k):
        source = inv_low if k < half else inv_high
        return source[(k % half) * BLOCK : (k % half + 1) * BLOCK, :]

    inv = []
    for k in range(0, nb, 2):
        x, y = inverse(k), inverse(k + 1)
        link = u[k * BLOCK : (k + 1) * BLOCK, (k + 1) * BLOCK : (k + 2) * BLOCK]
        low = -mm(mm(y, link, NT), x, NN)
        top = jnp.concatenate([x, jnp.zeros_like(x)], axis=1)
        inv.append(split(jnp.concatenate([top, jnp.concatenate([low, y], axis=1)], axis=0)))
    for away in range(nb):
        at = pl.multiple_of((lane + nb - away) % nb * BLOCK, BLOCK)
        work[:, pl.ds(at, BLOCK)] = a[away][...]
    first = (lax.axis_index("front") * lax.axis_size("row") + lax.axis_index("row")) * rows
    ri = first + lax.broadcasted_iota(jnp.int32, (rows, wide), 0)
    ci = lax.broadcasted_iota(jnp.int32, (rows, wide), 1)
    beyond = []
    for k in range(nb // 2):
        at = slice(k * wide, (k + 1) * wide)
        rest = slice((k + 1) * wide, None)
        m = mm3(split(work[:, at]), inv[k], NT)
        work[:, at] = m
        m_ref[:, at] = jnp.where(ri >= ci + k * wide, m, 0.0)
        if k + 1 < nb // 2:
            beyond.append(split(u[at, rest]))
            work[:, rest] -= mm3(split(m), beyond[k], NN)
    found = None
    for k in reversed(range(nb // 2)):
        at = slice(k * wide, (k + 1) * wide)
        x = work[:, at]
        if found is not None:
            x = x - mm3(found, beyond[k], NT)
        t = mm3(split(x), inv[k], NN)
        t_ref[:, at] = t
        th, tl = split(t)
        if found is None:
            found = (th, tl)
        else:
            found = tuple(jnp.concatenate(z, axis=1) for z in zip((th, tl), found))


def final_body(per_front, per_col, *refs):
    *tables, t, cols, spilt, base, out = refs
    step = pl.program_id(0)
    width = 2 * BLOCK

    @pl.when(step == 0)
    def _():
        out[...] = base[...]
        spill_add(per_front, per_col, 0, *tables, spilt, out)

    tt = split(t[:, pl.ds(pl.multiple_of(step * width, width), width)])
    chunk = 512
    for q in range(0, out.shape[1], chunk):
        other = jnp.concatenate([cols[0, q : q + chunk, :], cols[1, q : q + chunk, :]], axis=1)
        out[:, q : q + chunk] -= mm3(tt, split(other), NT)

    @pl.when(step == pl.num_programs(0) - 1)
    def _():
        top = lax.axis_index("front") * lax.axis_size("row") + lax.axis_index("row")

        @pl.when(top * out.shape[0] < LEADING)
        def _():
            out[...] = jnp.zeros_like(out)

        @pl.when(lax.axis_index("col") * out.shape[1] < LEADING)
        def _():
            out[:, :LEADING] = jnp.zeros((out.shape[0], LEADING), F32)


def from_lanes(parts, lanes):
    return parts[:1] + [
        lax.ppermute(parts[k], "col", [(i, (i + k) % lanes) for i in range(lanes)])
        for k in range(1, lanes)
    ]


def on_device(front_entries, child_updates, off, cnt):
    fronts = lax.axis_size("front")
    rows = lax.axis_size("row")
    cols = lax.axis_size("col")
    own_rows, own_cols = front_entries.shape
    owned = own_rows // BLOCK
    per_front = owned * rows
    per_col = own_cols // BLOCK
    r = lax.axis_index("row")
    c = lax.axis_index("col")
    row_blocks = off.shape[1] // rows
    block = (BLOCK, BLOCK)

    lead = call(
        lead_columns_body, "lead_columns", shape(cols, *block), [SMEM, SMEM, VMEM], VMEM
    )(off, cnt, child_updates)
    lead = lax.all_to_all(lead, "col", split_axis=0, concat_axis=0, tiled=True)
    strips = [front_entries[:, k * BLOCK : (k + 1) * BLOCK] for k in range(LEAD)]
    strip = jnp.where(c == 0, strips[0], 0.0)
    for k in range(1, cols):
        strip = strip + lax.ppermute(strips[k], "col", [(0, k)])
    share = own_rows // fronts
    part = jnp.where(lax.axis_index("front") == 0, strip[:share], 0.0)
    for k in range(1, fronts):
        part = part + lax.ppermute(strip[k * share : (k + 1) * share], "front", [(0, k)])
    lead = call(
        functools.partial(lead_rows_body, per_front),
        "lead_rows",
        shape(fronts, 4 * BLOCK + share, BLOCK),
        [SMEM, SMEM, VMEM, VMEM],
        VMEM,
    )(off, cnt, lead, part)
    early = lead
    lead = lax.all_to_all(lead, "front", split_axis=0, concat_axis=0, tiled=True)

    table = jax.ShapeDtypeStruct(off.shape, jnp.int32)
    line = jax.ShapeDtypeStruct((off.size,), jnp.int32)
    place, holder, items, pair, sizes = call(
        functools.partial(plan_body, per_col, cols),
        "plan",
        (table, table, line, line, jax.ShapeDtypeStruct((2,), jnp.int32)),
        [SMEM, SMEM, ANY],
        (SMEM,) * 5,
        [pltpu.SMEM((cols,), jnp.int32), pltpu.SMEM((cols * cols,), jnp.int32)],
    )(off, cnt, early)
    rest = call(
        far_columns_body,
        "far_columns",
        shape(cols, SLOTS, *block),
        [SMEM, ANY],
        ANY,
        [pltpu.SemaphoreType.DMA((off.shape[1],))],
        moved=4 << 20,
    )(place, child_updates)
    rest = from_lanes([rest[k : k + 1] for k in range(cols)], cols)
    rest = call(
        functools.partial(far_rows_body, per_front),
        "far_rows",
        shape(fronts, 2, SLOTS, *block),
        [SMEM, SMEM] + [VMEM] * cols,
        ANY,
        [pltpu.SemaphoreType.DMA((row_blocks,))],
        moved=8 << 20,
    )(off, cnt, *rest)

    piece, strip = call(
        functools.partial(pieces_body, per_front),
        "pieces",
        (shape(own_rows, BLOCK), shape(own_rows, BLOCK)),
        [SMEM, SMEM, VMEM, VMEM, ANY],
        (VMEM, VMEM),
    )(off, cnt, lead, strip, rest)
    near = lax.ppermute(piece, "row", [(0, 1), (1, 0)])
    side = lax.ppermute(piece, "row", [(0, 3), (1, 2)])
    far = lax.ppermute(piece, "row", [(0, 2), (1, 3)])
    upper = jnp.where(r == 0, piece, jnp.where(r == 1, near, jnp.where(r == 2, far, side)))
    lower = jnp.where(r == 1, piece, jnp.where(r == 0, near, jnp.where(r == 2, side, far)))
    corner = lax.all_gather(jnp.concatenate([upper, lower], axis=0), "col", axis=0)

    swap = [
        ((i * rows + j) * cols + k, (k * rows + j) * cols + i)
        for i in range(fronts)
        for j in range(rows)
        for k in range(cols)
    ]
    across = lax.ppermute(strip, ("front", "row", "col"), swap)
    mine = from_lanes([strip] * cols, cols)
    rest = lax.all_to_all(rest, "front", split_axis=0, concat_axis=0, tiled=True)
    s, inv_low = factor(0, LEAD // 2, True, corner, strip)
    s, inv_high = factor(LEAD // 2, LEAD // 2, False, s, across)
    across = lax.all_gather(across, ("front", "row"), axis=0)
    across = across.reshape(LEAD, own_cols, BLOCK)
    m, t = call(
        solve_body,
        "solve",
        (shape(own_rows, LEADING), shape(own_rows, LEADING)),
        [VMEM] * (3 + cols),
        (VMEM, VMEM),
        [pltpu.VMEM((own_rows, LEADING), F32)],
        flops=12 * 1150 * 10**6,
    )(s, inv_low, inv_high, *mine)

    tables = (off, cnt, place, items, pair, sizes)

    def spill(turn):
        spilt = call(
            functools.partial(spill_body, per_col),
            "spill",
            shape(cols, 2, *block),
            [SMEM] * 6 + [VMEM, ANY],
            VMEM,
        )(turn, off, place, items, pair, sizes, rest, t)
        return lax.all_to_all(spilt, "col", split_axis=0, concat_axis=0, tiled=True)

    def another(carry):
        turn, base = carry
        base = call(
            functools.partial(spill_add_body, per_front, per_col),
            "spill_add",
            shape(own_rows, own_cols),
            [SMEM] * 7 + [VMEM, VMEM],
            VMEM,
            input_output_aliases={8: 0},
        )(turn, *tables, spill(turn), base)
        return turn + 1, base

    whole = pl.BlockSpec((own_rows, own_cols), lambda i: (0, 0))
    assembled = pl.pallas_call(
        functools.partial(assemble_body, per_front, per_col),
        name="assemble",
        grid=(fronts // 2,),
        out_shape=shape(own_rows, own_cols),
        in_specs=[SMEM] * 3
        + [pl.BlockSpec((2, 2, SLOTS, *block), lambda i: (i, 0, 0, 0, 0)), whole],
        out_specs=whole,
        compiler_params=pltpu.CompilerParams(vmem_limit_bytes=48 << 20),
        cost_estimate=pl.CostEstimate(flops=0, bytes_accessed=12 << 20, transcendentals=0),
    )(off, cnt, holder, rest, front_entries)
    trailing = pl.pallas_call(
        functools.partial(final_body, per_front, per_col),
        name="final",
        grid=(LEAD // 2,),
        out_shape=shape(own_rows, own_cols),
        in_specs=[SMEM] * 6
        + [
            pl.BlockSpec((own_rows, LEADING), lambda i: (0, 0)),
            pl.BlockSpec((2, own_cols, BLOCK), lambda i: (i, 0, 0)),
            pl.BlockSpec((cols, 2, *block), lambda i: (0, 0, 0, 0)),
            whole,
        ],
        out_specs=whole,
        compiler_params=pltpu.CompilerParams(vmem_limit_bytes=56 << 20),
        cost_estimate=pl.CostEstimate(
            flops=12 * 1150 * 10**6, bytes_accessed=24 << 20, transcendentals=0
        ),
    )(*tables, t, across, spill(jnp.zeros((1,), jnp.int32)), assembled)
    _, trailing = lax.while_loop(
        lambda carry: carry[0][0] < sizes[1], another, (jnp.ones((1,), jnp.int32), trailing)
    )
    return trailing, m


def solution(mesh):
    placed = (P(("front", "row"), "col"), P("front", ("row", "col"), None), P(), P())
    return jax.shard_map(
        on_device,
        mesh=mesh,
        in_specs=placed,
        out_specs=(P(("front", "row"), "col"), P(("front", "row"), None)),
        check_vma=False,
    )
```

```python
import functools

import jax
import jax.numpy as jnp
from jax import lax
from jax.experimental import pallas as pl
from jax.experimental.pallas import tpu as pltpu
from jax.sharding import PartitionSpec as P

BLOCK = 128
LEAD = 8
LEADING = LEAD * BLOCK
SLOTS = 4
HIGHEST = lax.Precision.HIGHEST
NN = (((1,), (0,)), ((), ()))
NT = (((1,), (1,)), ((), ()))
TN = (((0,), (0,)), ((), ()))
F32 = jnp.float32
SMEM = pl.BlockSpec(memory_space=pltpu.SMEM)
VMEM = pl.BlockSpec(memory_space=pltpu.VMEM)
ANY = pl.BlockSpec(memory_space=pl.ANY)


def mm(a, b, dims):
    return lax.dot_general(a, b, dims, precision=HIGHEST, preferred_element_type=F32)


def split(x):
    high = x.astype(jnp.bfloat16)
    low = (x - high.astype(F32)).astype(jnp.bfloat16)
    return high, low


def mm3(a, b, dims):
    ah, al = a
    bh, bl = b
    dot = functools.partial(lax.dot_general, dimension_numbers=dims, preferred_element_type=F32)
    return dot(ah, bh) + (dot(al, bh) + dot(ah, bl))


def call(body, name, out_shape, in_specs, out_specs, scratch=(), flops=0, moved=0, **more):
    return pl.pallas_call(
        body,
        name=name,
        out_shape=out_shape,
        in_specs=in_specs,
        out_specs=out_specs,
        scratch_shapes=list(scratch),
        compiler_params=pltpu.CompilerParams(vmem_limit_bytes=48 << 20),
        cost_estimate=pl.CostEstimate(flops=flops, bytes_accessed=moved, transcendentals=0),
        **more,
    )


def shape(*dims):
    return jax.ShapeDtypeStruct(dims, F32)


def lead_columns_body(off, cnt, child, out):
    g = lax.axis_index("front")
    own = lax.axis_index("row") * lax.axis_size("col") + lax.axis_index("col")
    out[...] = jnp.zeros_like(out)
    live = cnt[g]
    for b in range(off.shape[1]):
        o = off[g, b]

        @pl.when((o < LEAD) & (b < live) & (own < live))
        def _():
            out[o] = child[0, :, b * BLOCK : (b + 1) * BLOCK]


def lead_rows_body(per_front, off, cnt, got, out):
    g = lax.axis_index("front")
    r = lax.axis_index("row")
    rows = got.shape[0]
    out[...] = jnp.zeros_like(out)
    for j in range(rows):
        f = off[g, r * rows + j] // per_front
        rank = jnp.int32(0)
        for i in range(j):
            rank += (off[g, r * rows + i] // per_front == f).astype(jnp.int32)
        out[f, rank] = got[j]


def piece_body(per_front, off, cnt, got, base, _, out):
    r = lax.axis_index("row")
    own = lax.axis_index("front")
    rows = off.shape[1] // lax.axis_size("row")
    owned = out.shape[0] // BLOCK
    out[...] = base[...]

    def child(g, carry):
        rank = jnp.int32(0)
        for j in range(rows):
            a = r * rows + j
            o = off[g, a]
            hit = o // per_front == own
            at = pl.ds(pl.multiple_of((o % owned) * BLOCK, BLOCK), BLOCK)
            here = rank

            @pl.when(hit & (a < cnt[g]))
            def _():
                out[at, :] += got[g, here]

            rank += hit.astype(jnp.int32)
        return carry

    lax.fori_loop(0, got.shape[0], child, 0)


def plan_body(
    per_col, lanes, off, cnt, _, place, holder, items, pair, sizes, taken, pairs, swap
):
    children, blocks = off.shape
    for i in range(lanes * lanes):
        pairs[i] = 0
    sizes[0] = 0
    sizes[1] = 0

    def child(g, carry):
        for m in range(lanes):
            taken[m] = 0
        for b in range(blocks):
            holder[g, b] = -1
        first = sizes[0]
        live = cnt[g]

        def own_lane(b, n):
            o = off[g, b]
            c = o // per_col
            k = taken[c]
            use = (o >= LEAD) & (b < live)
            fits = use & (k < SLOTS)
            at = c * SLOTS + k
            place[g, b] = jnp.where(fits, at, -1)
            holder[g, jnp.where(fits, at, blocks)] = b
            taken[c] = k + fits.astype(jnp.int32)
            items[n] = g * blocks + b
            return n + (use & (k >= SLOTS)).astype(jnp.int32)

        last = lax.fori_loop(0, blocks, own_lane, first, unroll=4)
        sizes[0] = last

        def other_lane(n, carry):
            b = items[n] % blocks
            c = off[g, b] // per_col
            best = jnp.int32(1 << 20)
            lane = jnp.int32(0)
            for m in range(lanes):
                score = jnp.where(taken[m] < SLOTS, pairs[m * lanes + c], 1 << 20)
                lane = jnp.where(score < best, m, lane)
                best = jnp.minimum(score, best)

            def put(n, b, lane, c):
                place[g, b] = lane * SLOTS + taken[lane]
                pair[n] = pairs[lane * lanes + c]
                taken[lane] += 1
                pairs[lane * lanes + c] += 1
                sizes[1] = jnp.maximum(sizes[1], pairs[lane * lanes + c])

            swap[0] = -1
            swap[1] = -1

            @pl.when(best > 0)
            def _():
                via = jnp.int32(-1)
                to = jnp.int32(-1)
                for m in range(lanes):
                    for v in range(lanes):
                        if v != m:
                            own = holder[g, v * SLOTS]
                            ok = (via < 0) & (own >= 0) & (v != c) & (m != c)
                            ok &= (taken[m] < SLOTS) & (pairs[m * lanes + v] == 0)
                            ok &= pairs[v * lanes + c] == 0
                            via = jnp.where(ok, v, via)
                            to = jnp.where(ok, m, to)
                swap[0] = via
                swap[1] = to

            via = swap[0]
            to = swap[1]

            @pl.when(via < 0)
            def _():
                put(n, b, lane, c)

            @pl.when(via >= 0)
            def _():
                own = holder[g, via * SLOTS]
                holder[g, via * SLOTS] = -1
                more = sizes[0]
                sizes[0] = more + 1
                items[more] = g * blocks + own
                put(more, own, to, via)
                place[g, b] = via * SLOTS
                pair[n] = 0
                pairs[via * lanes + c] = 1
                sizes[1] = jnp.maximum(sizes[1], 1)

            return carry

        lax.fori_loop(first, last, other_lane, 0)
        return carry

    lax.fori_loop(0, children, child, 0)


def far_columns_body(place, child, out, sems):
    g = lax.axis_index("front")
    c = lax.axis_index("col")
    lanes = out.shape[0]
    copies = []
    for b in range(place.shape[1]):
        p = place[g, b]
        to = jnp.maximum(p, 0)
        copy = pltpu.make_async_copy(
            child.at[0, :, pl.ds(b * BLOCK, BLOCK)],
            out.at[(to // SLOTS + lanes - c) % lanes, to % SLOTS],
            sems.at[b],
        )
        copies.append((p >= 0, copy))

        @pl.when(p >= 0)
        def _():
            copy.start()

    for use, copy in copies:

        @pl.when(use)
        def _():
            copy.wait()


def far_rows_body(per_front, off, cnt, *refs):
    *got, out, sems = refs
    g = lax.axis_index("front")
    r = lax.axis_index("row")
    c = lax.axis_index("col")
    rows = len(got)
    copies = []
    for away in range(rows):
        j = (c + rows - away) % rows
        a = r * rows + j
        o = off[g, a]
        f = o // per_front
        rank = jnp.int32(0)
        for i in range(rows):
            rank += ((off[g, r * rows + i] // per_front == f) & (i < j)).astype(jnp.int32)
        use = (o >= LEAD) & (a < cnt[g])
        copy = pltpu.make_async_copy(
            got[away].at[0], out.at[f, jnp.minimum(rank, 1)], sems.at[away]
        )
        copies.append((use, copy))

        @pl.when(use)
        def _():
            copy.start()

    for use, copy in copies:

        @pl.when(use)
        def _():
            copy.wait()


def spill_body(per_col, turn, off, place, items, pair, sizes, got, _, out):
    c = lax.axis_index("col")
    out[...] = jnp.zeros_like(out)
    blocks = off.shape[1]

    def item(n, carry):
        g = items[n] // blocks
        b = items[n] % blocks
        p = place[g, b]

        @pl.when((pair[n] == turn[0]) & (p // SLOTS == c))
        def _():
            out[off[g, b] // per_col] = got[g, :, p % SLOTS]

        return carry

    lax.fori_loop(0, sizes[0], item, 0)


def each_row(per_front, g, off, cnt, add):
    f = lax.axis_index("front")
    r = lax.axis_index("row")
    rows = off.shape[1] // lax.axis_size("row")
    owned = per_front // lax.axis_size("row")
    rank = jnp.int32(0)
    for j in range(rows):
        a = r * rows + j
        o = off[g, a]
        hit = o // per_front == f
        row = pl.ds(pl.multiple_of((o % owned) * BLOCK, BLOCK), BLOCK)
        here = rank

        @pl.when(hit & (a < cnt[g]) & (o >= LEAD))
        def _():
            add(row, here)

        rank += hit.astype(jnp.int32)


def own_column(per_col, p):
    return pl.ds(pl.multiple_of((p % per_col) * BLOCK, BLOCK), BLOCK)


def spill_add(per_front, per_col, turn, off, cnt, place, items, pair, sizes, spilt, out):
    c = lax.axis_index("col")
    blocks = off.shape[1]

    def item(n, carry):
        g = items[n] // blocks
        b = items[n] % blocks
        p = off[g, b]
        lane = jnp.maximum(place[g, b], 0) // SLOTS

        @pl.when((pair[n] == turn) & (p // per_col == c))
        def _():
            def add(row, rank):
                out[row, own_column(per_col, p)] += spilt[lane, rank]

            each_row(per_front, g, off, cnt, add)

        return carry

    lax.fori_loop(0, sizes[0], item, 0)


def spill_add_body(per_front, per_col, turn, off, cnt, place, items, pair, sizes, spilt, base, out):
    out[...] = base[...]
    spill_add(per_front, per_col, turn[0], off, cnt, place, items, pair, sizes, spilt, out)


def assemble_body(per_front, per_col, off, cnt, holder, got, base, _, out):
    c = lax.axis_index("col")
    step = pl.program_id(0)

    @pl.when(step == 0)
    def _():
        out[...] = base[...]

    for half in range(got.shape[0]):
        g = got.shape[0] * step + half

        def add(row, rank):
            for k in range(SLOTS):
                b = holder[g, c * SLOTS + k]

                @pl.when(b >= 0)
                def _():
                    at = own_column(per_col, off[g, jnp.maximum(b, 0)])
                    out[row, at] += got[half, rank, k]

        each_row(per_front, g, off, cnt, add)


def gate_body(piece, near, side, far, corner):
    r = lax.axis_index("row")
    half = piece.shape[0]
    for k, (upper, lower) in enumerate(((piece, near), (near, piece), (far, side), (side, far))):

        @pl.when(r == k)
        def _():
            corner[:half] = upper[...]
            corner[half:] = lower[...]


def after_body(x, *refs):
    refs[-1][...] = x[...]


def after(x, *others):
    return call(
        after_body, "after", shape(*x.shape), [VMEM] + [ANY] * len(others), VMEM, moved=8 * x.size
    )(x, *others)


def factor_block(w):
    sub = lax.broadcasted_iota(jnp.int32, (8, BLOCK), 0)
    for lo in range(0, BLOCK, 8):
        r0 = w[lo : lo + 8, 0:BLOCK]
        r1 = w[lo : lo + 8, BLOCK : 2 * BLOCK]
        e = [jnp.broadcast_to(r0[:, lo + k : lo + k + 1], (8, BLOCK)) for k in range(8)]
        recip, across, top0, top1 = [], {}, [], []
        pivots = jnp.ones((8, BLOCK), F32)
        for i in range(8):
            row = {k: jnp.broadcast_to(e[k][i : i + 1, :], (8, BLOCK)) for k in range(i, 8)}
            inv = 1.0 / row[i]
            recip.append(inv)
            m = jnp.where(sub > i, e[i] * inv, 0.0)
            b0 = jnp.broadcast_to(r0[i : i + 1, :], (8, BLOCK))
            b1 = jnp.broadcast_to(r1[i : i + 1, :], (8, BLOCK))
            top0.append(b0)
            top1.append(b1)
            for k in range(i + 1, 8):
                across[i, k] = row[k]
                e[k] = e[k] - m * row[k]
            r0 = r0 - m * b0
            r1 = r1 - m * b1
            pivots = jnp.where(sub == i, row[i], pivots)
        scale = lax.rsqrt(pivots)
        w[lo : lo + 8, 0:BLOCK] = r0 * scale
        w[lo : lo + 8, BLOCK : 2 * BLOCK] = r1 * scale
        q = lo + 8
        while q < BLOCK:
            n = min(32, BLOCK - q)

            def tall(x):
                return jnp.concatenate([x] * (n // 8), axis=0) if n > 8 else x

            g0 = w[q : q + n, 0:BLOCK]
            g1 = w[q : q + n, BLOCK : 2 * BLOCK]
            e = [jnp.broadcast_to(g0[:, lo + k : lo + k + 1], (n, BLOCK)) for k in range(8)]
            for i in range(8):
                m = e[i] * tall(recip[i])
                for k in range(i + 1, 8):
                    e[k] = e[k] - m * tall(across[i, k])
                g0 = g0 - m * tall(top0[i])
                g1 = g1 - m * tall(top1[i])
            w[q : q + n, 0:BLOCK] = g0
            w[q : q + n, BLOCK : 2 * BLOCK] = g1
            q += n


def factor_body(start, blocks, fresh, a, _, s, inv_ref, w):
    ri = lax.broadcasted_iota(jnp.int32, (BLOCK, BLOCK), 0)
    ci = lax.broadcasted_iota(jnp.int32, (BLOCK, BLOCK), 1)
    eye = (ri == ci).astype(F32)
    if fresh:
        for c in range(LEAD):
            s[:, c * BLOCK : (c + 1) * BLOCK] = a[c]
    else:
        s[...] = a[...]

    def step(k, carry):
        at = pl.ds(pl.multiple_of(k * BLOCK, BLOCK), BLOCK)
        w[:, 0:BLOCK] = s[at, at]
        w[:, BLOCK : 2 * BLOCK] = eye
        factor_block(w)
        inverse = jnp.where(ri >= ci, w[:, BLOCK : 2 * BLOCK], 0.0)
        inv_ref[pl.ds(pl.multiple_of((k - start) * BLOCK, BLOCK), BLOCK), :] = inverse
        for kk in range(start, min(start + blocks, LEAD - 1)):

            @pl.when(k == kk)
            def _():
                h = (kk + 1) * BLOCK
                u = mm(inverse, s[kk * BLOCK : h, h:], NN)
                s[kk * BLOCK : h, h:] = u
                for i in range(kk + 1, LEAD):
                    o = (i - kk - 1) * BLOCK
                    s[i * BLOCK : (i + 1) * BLOCK, i * BLOCK :] -= mm(
                        u[:, o : o + BLOCK], u[:, o:], TN
                    )

        return carry

    lax.fori_loop(start, start + blocks, step, 0)


def factor(start, blocks, fresh, a, after):
    return call(
        functools.partial(factor_body, start, blocks, fresh),
        "factor",
        (shape(LEADING, LEADING), shape(blocks * BLOCK, BLOCK)),
        [VMEM, ANY],
        (VMEM, VMEM),
        [pltpu.VMEM((BLOCK, 2 * BLOCK), F32)],
        flops=20 * 1150 * 10**6,
    )(a, after)


def solve_body(u, inv_low, inv_high, *refs):
    *a, m_ref, t_ref, work = refs
    nb = len(a)
    rows = a[0].shape[0]
    half = nb // 2
    lane = lax.axis_index("col")
    wide = 2 * BLOCK

    def inverse(k):
        source = inv_low if k < half else inv_high
        return source[(k % half) * BLOCK : (k % half + 1) * BLOCK, :]

    inv = []
    for k in range(0, nb, 2):
        x, y = inverse(k), inverse(k + 1)
        link = u[k * BLOCK : (k + 1) * BLOCK, (k + 1) * BLOCK : (k + 2) * BLOCK]
        low = -mm(mm(y, link, NT), x, NN)
        top = jnp.concatenate([x, jnp.zeros_like(x)], axis=1)
        inv.append(split(jnp.concatenate([top, jnp.concatenate([low, y], axis=1)], axis=0)))
    for away in range(nb):
        at = pl.multiple_of((lane + nb - away) % nb * BLOCK, BLOCK)
        work[:, pl.ds(at, BLOCK)] = a[away][...]
    first = (lax.axis_index("front") * lax.axis_size("row") + lax.axis_index("row")) * rows
    ri = first + lax.broadcasted_iota(jnp.int32, (rows, wide), 0)
    ci = lax.broadcasted_iota(jnp.int32, (rows, wide), 1)
    beyond = []
    for k in range(nb // 2):
        at = slice(k * wide, (k + 1) * wide)
        rest = slice((k + 1) * wide, None)
        m = mm3(split(work[:, at]), inv[k], NT)
        work[:, at] = m
        m_ref[:, at] = jnp.where(ri >= ci + k * wide, m, 0.0)
        if k + 1 < nb // 2:
            beyond.append(split(u[at, rest]))
            work[:, rest] -= mm3(split(m), beyond[k], NN)
    found = None
    for k in reversed(range(nb // 2)):
        at = slice(k * wide, (k + 1) * wide)
        x = work[:, at]
        if found is not None:
            x = x - mm3(found, beyond[k], NT)
        t = mm3(split(x), inv[k], NN)
        t_ref[:, at] = t
        th, tl = split(t)
        if found is None:
            found = (th, tl)
        else:
            found = tuple(jnp.concatenate(z, axis=1) for z in zip((th, tl), found))


def final_body(per_front, per_col, *refs):
    *tables, t, cols, spilt, base, out = refs
    step = pl.program_id(0)
    width = 2 * BLOCK

    @pl.when(step == 0)
    def _():
        out[...] = base[...]
        spill_add(per_front, per_col, 0, *tables, spilt, out)

    tt = split(t[:, pl.ds(pl.multiple_of(step * width, width), width)])
    chunk = 512
    for q in range(0, out.shape[1], chunk):
        other = jnp.concatenate([cols[0, q : q + chunk, :], cols[1, q : q + chunk, :]], axis=1)
        out[:, q : q + chunk] -= mm3(tt, split(other), NT)

    @pl.when(step == pl.num_programs(0) - 1)
    def _():
        top = lax.axis_index("front") * lax.axis_size("row") + lax.axis_index("row")

        @pl.when(top * out.shape[0] < LEADING)
        def _():
            out[...] = jnp.zeros_like(out)

        @pl.when(lax.axis_index("col") * out.shape[1] < LEADING)
        def _():
            out[:, :LEADING] = jnp.zeros((out.shape[0], LEADING), F32)


def from_lanes(parts, lanes):
    return parts[:1] + [
        lax.ppermute(parts[k], "col", [(i, (i + k) % lanes) for i in range(lanes)])
        for k in range(1, lanes)
    ]


def on_device(front_entries, child_updates, off, cnt):
    fronts = lax.axis_size("front")
    rows = lax.axis_size("row")
    cols = lax.axis_size("col")
    own_rows, own_cols = front_entries.shape
    owned = own_rows // BLOCK
    per_front = owned * rows
    per_col = own_cols // BLOCK
    r = lax.axis_index("row")
    c = lax.axis_index("col")
    row_blocks = off.shape[1] // rows
    block = (BLOCK, BLOCK)

    lead = call(
        lead_columns_body, "lead_columns", shape(cols, *block), [SMEM, SMEM, VMEM], VMEM
    )(off, cnt, child_updates)
    lead = lax.all_to_all(lead, "col", split_axis=0, concat_axis=0, tiled=True)
    strips = [front_entries[:, k * BLOCK : (k + 1) * BLOCK] for k in range(LEAD)]
    strip = jnp.where(c == 0, strips[0], 0.0)
    for k in range(1, cols):
        strip = strip + lax.ppermute(strips[k], "col", [(0, k)])
    lead = call(
        functools.partial(lead_rows_body, per_front),
        "lead_rows",
        shape(fronts, 2, *block),
        [SMEM, SMEM, VMEM],
        VMEM,
    )(off, cnt, lead)
    early = lead
    lead = lax.all_to_all(lead, "front", split_axis=0, concat_axis=0, tiled=True)

    table = jax.ShapeDtypeStruct(off.shape, jnp.int32)
    line = jax.ShapeDtypeStruct((off.size,), jnp.int32)
    place, holder, items, pair, sizes = call(
        functools.partial(plan_body, per_col, cols),
        "plan",
        (
            table,
            jax.ShapeDtypeStruct((off.shape[0], off.shape[1] + 1), jnp.int32),
            jax.ShapeDtypeStruct((off.size + 1,), jnp.int32),
            line,
            jax.ShapeDtypeStruct((2,), jnp.int32),
        ),
        [SMEM, SMEM, ANY],
        (SMEM,) * 5,
        [pltpu.SMEM((n,), jnp.int32) for n in (cols, cols * cols, 2)],
    )(off, cnt, early)
    rest = call(
        far_columns_body,
        "far_columns",
        shape(cols, SLOTS, *block),
        [SMEM, ANY],
        ANY,
        [pltpu.SemaphoreType.DMA((off.shape[1],))],
        moved=4 << 20,
    )(place, child_updates)
    planned = rest
    parts = from_lanes([rest[k : k + 1] for k in range(cols)], cols)
    rest = call(
        functools.partial(far_rows_body, per_front),
        "far_rows",
        shape(fronts, 2, SLOTS, *block),
        [SMEM, SMEM] + [VMEM] * cols,
        ANY,
        [pltpu.SemaphoreType.DMA((row_blocks,))],
        moved=8 << 20,
    )(off, cnt, *parts)

    strip = call(
        functools.partial(piece_body, per_front),
        "piece",
        shape(own_rows, BLOCK),
        [SMEM, SMEM, VMEM, VMEM, ANY],
        VMEM,
    )(off, cnt, lead, strip, planned)

    swap = [
        ((i * rows + j) * cols + k, (k * rows + j) * cols + i)
        for i in range(fronts)
        for j in range(rows)
        for k in range(cols)
    ]
    across = lax.ppermute(strip, ("front", "row", "col"), swap)

    piece = jnp.where(lax.axis_index("front") == 0, strip, 0.0)
    for k in range(2, fronts, 2):
        piece = piece + lax.ppermute(strip, "front", [(0, k)])
    odd = lax.ppermute(piece, "front", [(k, k + 1) for k in range(0, fronts, 2)])
    piece = after(piece + odd, across, *parts[1:])
    near = lax.ppermute(piece, "row", [(0, 1), (1, 0)])
    side = lax.ppermute(piece, "row", [(0, 3), (1, 2)])
    far = lax.ppermute(piece, "row", [(0, 2), (1, 3)])
    corner = call(
        gate_body, "gate", shape(2 * own_rows, BLOCK), [VMEM] * 4, VMEM
    )(piece, near, side, far)

    across = after(across, corner)
    corner = lax.all_gather(corner, "col", axis=0)
    across = lax.all_gather(across, ("front", "row"), axis=0)
    across = across.reshape(LEAD, own_cols, BLOCK)
    rest = lax.all_to_all(rest, "front", split_axis=0, concat_axis=0, tiled=True)
    s, inv_low = factor(0, LEAD // 2, True, corner, strip)
    mine = from_lanes([after(strip, inv_low)] * cols, cols)
    s, inv_high = factor(LEAD // 2, LEAD // 2, False, s, strip)
    m, t = call(
        solve_body,
        "solve",
        (shape(own_rows, LEADING), shape(own_rows, LEADING)),
        [VMEM] * (3 + cols),
        (VMEM, VMEM),
        [pltpu.VMEM((own_rows, LEADING), F32)],
        flops=12 * 1150 * 10**6,
    )(s, inv_low, inv_high, *mine)

    tables = (off, cnt, place, items, pair, sizes)

    def spill(turn):
        spilt = call(
            functools.partial(spill_body, per_col),
            "spill",
            shape(cols, 2, *block),
            [SMEM] * 6 + [VMEM, ANY],
            VMEM,
        )(turn, off, place, items, pair, sizes, rest, inv_high)
        return lax.all_to_all(spilt, "col", split_axis=0, concat_axis=0, tiled=True)

    def another(carry):
        turn, base = carry
        base = call(
            functools.partial(spill_add_body, per_front, per_col),
            "spill_add",
            shape(own_rows, own_cols),
            [SMEM] * 7 + [VMEM, VMEM],
            VMEM,
            input_output_aliases={8: 0},
        )(turn, *tables, spill(turn), base)
        return turn + 1, base

    whole = pl.BlockSpec((own_rows, own_cols), lambda i: (0, 0))
    assembled = pl.pallas_call(
        functools.partial(assemble_body, per_front, per_col),
        name="assemble",
        grid=(fronts // 2,),
        out_shape=shape(own_rows, own_cols),
        in_specs=[SMEM] * 3
        + [pl.BlockSpec((2, 2, SLOTS, *block), lambda i: (i, 0, 0, 0, 0)), whole, ANY],
        out_specs=whole,
        compiler_params=pltpu.CompilerParams(vmem_limit_bytes=48 << 20),
        cost_estimate=pl.CostEstimate(flops=0, bytes_accessed=12 << 20, transcendentals=0),
    )(off, cnt, holder, rest, front_entries, inv_high)
    trailing = pl.pallas_call(
        functools.partial(final_body, per_front, per_col),
        name="final",
        grid=(LEAD // 2,),
        out_shape=shape(own_rows, own_cols),
        in_specs=[SMEM] * 6
        + [
            pl.BlockSpec((own_rows, LEADING), lambda i: (0, 0)),
            pl.BlockSpec((2, own_cols, BLOCK), lambda i: (i, 0, 0)),
            pl.BlockSpec((cols, 2, *block), lambda i: (0, 0, 0, 0)),
            whole,
        ],
        out_specs=whole,
        compiler_params=pltpu.CompilerParams(vmem_limit_bytes=56 << 20),
        cost_estimate=pl.CostEstimate(
            flops=12 * 1150 * 10**6, bytes_accessed=24 << 20, transcendentals=0
        ),
    )(*tables, t, across, spill(jnp.zeros((1,), jnp.int32)), assembled)
    _, trailing = lax.while_loop(
        lambda carry: carry[0][0] < sizes[1], another, (jnp.ones((1,), jnp.int32), trailing)
    )
    return trailing, m


def solution(mesh):
    placed = (P(("front", "row"), "col"), P("front", ("row", "col"), None), P(), P())
    return jax.shard_map(
        on_device,
        mesh=mesh,
        in_specs=placed,
        out_specs=(P(("front", "row"), "col"), P(("front", "row"), None)),
        check_vma=False,
    )
```

```python
import functools

import jax
import jax.numpy as jnp
from jax import lax
from jax.experimental import pallas as pl
from jax.experimental.pallas import tpu as pltpu
from jax.sharding import PartitionSpec as P

BLOCK = 128
LEAD = 8
LEADING = LEAD * BLOCK
SLOTS = 4
HIGHEST = lax.Precision.HIGHEST
NN = (((1,), (0,)), ((), ()))
NT = (((1,), (1,)), ((), ()))
TN = (((0,), (0,)), ((), ()))
F32 = jnp.float32
SMEM = pl.BlockSpec(memory_space=pltpu.SMEM)
VMEM = pl.BlockSpec(memory_space=pltpu.VMEM)
ANY = pl.BlockSpec(memory_space=pl.ANY)


def mm(a, b, dims):
    return lax.dot_general(a, b, dims, precision=HIGHEST, preferred_element_type=F32)


def split(x):
    high = x.astype(jnp.bfloat16)
    low = (x - high.astype(F32)).astype(jnp.bfloat16)
    return high, low


def mm3(a, b, dims):
    ah, al = a
    bh, bl = b
    dot = functools.partial(lax.dot_general, dimension_numbers=dims, preferred_element_type=F32)
    return dot(ah, bh) + (dot(al, bh) + dot(ah, bl))


def call(body, name, out_shape, in_specs, out_specs, scratch=(), flops=0, moved=0, **more):
    return pl.pallas_call(
        body,
        name=name,
        out_shape=out_shape,
        in_specs=in_specs,
        out_specs=out_specs,
        scratch_shapes=list(scratch),
        compiler_params=pltpu.CompilerParams(vmem_limit_bytes=48 << 20),
        cost_estimate=pl.CostEstimate(flops=flops, bytes_accessed=moved, transcendentals=0),
        **more,
    )


def shape(*dims):
    return jax.ShapeDtypeStruct(dims, F32)


def lead_columns_body(off, cnt, child, out):
    g = lax.axis_index("front")
    own = lax.axis_index("row") * lax.axis_size("col") + lax.axis_index("col")
    out[...] = jnp.zeros_like(out)
    live = cnt[g]
    for b in range(off.shape[1]):
        o = off[g, b]

        @pl.when((o < LEAD) & (b < live) & (own < live))
        def _():
            out[o] = child[0, :, b * BLOCK : (b + 1) * BLOCK]


def lead_rows_body(per_front, off, cnt, got, out):
    g = lax.axis_index("front")
    r = lax.axis_index("row")
    rows = got.shape[0]
    out[...] = jnp.zeros_like(out)
    for j in range(rows):
        f = off[g, r * rows + j] // per_front
        rank = jnp.int32(0)
        for i in range(j):
            rank += (off[g, r * rows + i] // per_front == f).astype(jnp.int32)
        out[f, rank] = got[j]


def piece_body(per_front, off, cnt, got, base, _, out):
    r = lax.axis_index("row")
    own = lax.axis_index("front")
    rows = off.shape[1] // lax.axis_size("row")
    owned = out.shape[0] // BLOCK
    out[...] = base[...]

    def child(g, carry):
        rank = jnp.int32(0)
        for j in range(rows):
            a = r * rows + j
            o = off[g, a]
            hit = o // per_front == own
            at = pl.ds(pl.multiple_of((o % owned) * BLOCK, BLOCK), BLOCK)
            here = rank

            @pl.when(hit & (a < cnt[g]))
            def _():
                out[at, :] += got[g, here]

            rank += hit.astype(jnp.int32)
        return carry

    lax.fori_loop(0, got.shape[0], child, 0)


def plan_body(
    per_col, lanes, off, cnt, _, place, holder, items, pair, sizes, taken, pairs, swap
):
    children, blocks = off.shape
    for i in range(lanes * lanes):
        pairs[i] = 0
    sizes[0] = 0
    sizes[1] = 0

    def child(g, carry):
        for m in range(lanes):
            taken[m] = 0
        for b in range(blocks):
            holder[g, b] = -1
        first = sizes[0]
        live = cnt[g]

        def own_lane(b, n):
            o = off[g, b]
            c = o // per_col
            k = taken[c]
            use = (o >= LEAD) & (b < live)
            fits = use & (k < SLOTS)
            at = c * SLOTS + k
            place[g, b] = jnp.where(fits, at, -1)
            holder[g, jnp.where(fits, at, blocks)] = b
            taken[c] = k + fits.astype(jnp.int32)
            items[n] = g * blocks + b
            return n + (use & (k >= SLOTS)).astype(jnp.int32)

        last = lax.fori_loop(0, blocks, own_lane, first, unroll=4)
        sizes[0] = last

        def other_lane(n, carry):
            b = items[n] % blocks
            c = off[g, b] // per_col
            best = jnp.int32(1 << 20)
            lane = jnp.int32(0)
            for m in range(lanes):
                score = jnp.where(taken[m] < SLOTS, pairs[m * lanes + c], 1 << 20)
                lane = jnp.where(score < best, m, lane)
                best = jnp.minimum(score, best)

            def put(n, b, lane, c):
                place[g, b] = lane * SLOTS + taken[lane]
                pair[n] = pairs[lane * lanes + c]
                taken[lane] += 1
                pairs[lane * lanes + c] += 1
                sizes[1] = jnp.maximum(sizes[1], pairs[lane * lanes + c])

            swap[0] = -1
            swap[1] = -1

            @pl.when(best > 0)
            def _():
                via = jnp.int32(-1)
                to = jnp.int32(-1)
                for m in range(lanes):
                    for v in range(lanes):
                        if v != m:
                            own = holder[g, v * SLOTS]
                            ok = (via < 0) & (own >= 0) & (v != c) & (m != c)
                            ok &= (taken[m] < SLOTS) & (pairs[m * lanes + v] == 0)
                            ok &= pairs[v * lanes + c] == 0
                            via = jnp.where(ok, v, via)
                            to = jnp.where(ok, m, to)
                swap[0] = via
                swap[1] = to

            via = swap[0]
            to = swap[1]

            @pl.when(via < 0)
            def _():
                put(n, b, lane, c)

            @pl.when(via >= 0)
            def _():
                own = holder[g, via * SLOTS]
                holder[g, via * SLOTS] = -1
                more = sizes[0]
                sizes[0] = more + 1
                items[more] = g * blocks + own
                put(more, own, to, via)
                place[g, b] = via * SLOTS
                pair[n] = 0
                pairs[via * lanes + c] = 1
                sizes[1] = jnp.maximum(sizes[1], 1)

            return carry

        lax.fori_loop(first, last, other_lane, 0)
        return carry

    lax.fori_loop(0, children, child, 0)


def far_columns_body(place, child, out, sems):
    g = lax.axis_index("front")
    c = lax.axis_index("col")
    lanes = out.shape[0]
    copies = []
    for b in range(place.shape[1]):
        p = place[g, b]
        to = jnp.maximum(p, 0)
        copy = pltpu.make_async_copy(
            child.at[0, :, pl.ds(b * BLOCK, BLOCK)],
            out.at[(to // SLOTS + lanes - c) % lanes, to % SLOTS],
            sems.at[b],
        )
        copies.append((p >= 0, copy))

        @pl.when(p >= 0)
        def _():
            copy.start()

    for use, copy in copies:

        @pl.when(use)
        def _():
            copy.wait()


def far_rows_body(per_front, off, cnt, *refs):
    *got, out, sems = refs
    g = lax.axis_index("front")
    r = lax.axis_index("row")
    c = lax.axis_index("col")
    rows = len(got)
    copies = []
    for away in range(rows):
        j = (c + rows - away) % rows
        a = r * rows + j
        o = off[g, a]
        f = o // per_front
        rank = jnp.int32(0)
        for i in range(rows):
            rank += ((off[g, r * rows + i] // per_front == f) & (i < j)).astype(jnp.int32)
        use = (o >= LEAD) & (a < cnt[g])
        copy = pltpu.make_async_copy(
            got[away].at[0], out.at[f, jnp.minimum(rank, 1)], sems.at[away]
        )
        copies.append((use, copy))

        @pl.when(use)
        def _():
            copy.start()

    for use, copy in copies:

        @pl.when(use)
        def _():
            copy.wait()


def spill_body(per_col, turn, off, place, items, pair, sizes, got, _, out):
    c = lax.axis_index("col")
    out[...] = jnp.zeros_like(out)
    blocks = off.shape[1]

    def item(n, carry):
        g = items[n] // blocks
        b = items[n] % blocks
        p = place[g, b]

        @pl.when((pair[n] == turn[0]) & (p // SLOTS == c))
        def _():
            out[off[g, b] // per_col] = got[g, :, p % SLOTS]

        return carry

    lax.fori_loop(0, sizes[0], item, 0)


def each_row(per_front, g, off, cnt, add):
    f = lax.axis_index("front")
    r = lax.axis_index("row")
    rows = off.shape[1] // lax.axis_size("row")
    owned = per_front // lax.axis_size("row")
    rank = jnp.int32(0)
    for j in range(rows):
        a = r * rows + j
        o = off[g, a]
        hit = o // per_front == f
        row = pl.ds(pl.multiple_of((o % owned) * BLOCK, BLOCK), BLOCK)
        here = rank

        @pl.when(hit & (a < cnt[g]) & (o >= LEAD))
        def _():
            add(row, here)

        rank += hit.astype(jnp.int32)


def own_column(per_col, p):
    return pl.ds(pl.multiple_of((p % per_col) * BLOCK, BLOCK), BLOCK)


def spill_add(per_front, per_col, turn, off, cnt, place, items, pair, sizes, spilt, out):
    c = lax.axis_index("col")
    blocks = off.shape[1]

    def item(n, carry):
        g = items[n] // blocks
        b = items[n] % blocks
        p = off[g, b]
        lane = jnp.maximum(place[g, b], 0) // SLOTS

        @pl.when((pair[n] == turn) & (p // per_col == c))
        def _():
            def add(row, rank):
                out[row, own_column(per_col, p)] += spilt[lane, rank]

            each_row(per_front, g, off, cnt, add)

        return carry

    lax.fori_loop(0, sizes[0], item, 0)


def spill_add_body(per_front, per_col, turn, off, cnt, place, items, pair, sizes, spilt, base, out):
    out[...] = base[...]
    spill_add(per_front, per_col, turn[0], off, cnt, place, items, pair, sizes, spilt, out)


def assemble_body(per_front, per_col, off, cnt, holder, got, base, _, out):
    c = lax.axis_index("col")
    step = pl.program_id(0)

    @pl.when(step == 0)
    def _():
        out[...] = base[...]

    for half in range(got.shape[0]):
        g = got.shape[0] * step + half

        def add(row, rank):
            for k in range(SLOTS):
                b = holder[g, c * SLOTS + k]

                @pl.when(b >= 0)
                def _():
                    at = own_column(per_col, off[g, jnp.maximum(b, 0)])
                    out[row, at] += got[half, rank, k]

        each_row(per_front, g, off, cnt, add)


def gate_body(piece, near, side, far, corner):
    r = lax.axis_index("row")
    half = piece.shape[0]
    for k, (upper, lower) in enumerate(((piece, near), (near, piece), (far, side), (side, far))):

        @pl.when(r == k)
        def _():
            corner[:half] = upper[...]
            corner[half:] = lower[...]


def after_body(x, *refs):
    refs[-1][...] = x[...]


def after(x, *others):
    return call(
        after_body, "after", shape(*x.shape), [VMEM] + [ANY] * len(others), VMEM, moved=8 * x.size
    )(x, *others)


def factor_block(w):
    sub = lax.broadcasted_iota(jnp.int32, (8, BLOCK), 0)
    for lo in range(0, BLOCK, 8):
        r0 = w[lo : lo + 8, 0:BLOCK]
        r1 = w[lo : lo + 8, BLOCK : 2 * BLOCK]
        e = [jnp.broadcast_to(r0[:, lo + k : lo + k + 1], (8, BLOCK)) for k in range(8)]
        recip, across, top0, top1 = [], {}, [], []
        pivots = jnp.ones((8, BLOCK), F32)
        for i in range(8):
            row = {k: jnp.broadcast_to(e[k][i : i + 1, :], (8, BLOCK)) for k in range(i, 8)}
            inv = 1.0 / row[i]
            recip.append(inv)
            m = jnp.where(sub > i, e[i] * inv, 0.0)
            b0 = jnp.broadcast_to(r0[i : i + 1, :], (8, BLOCK))
            b1 = jnp.broadcast_to(r1[i : i + 1, :], (8, BLOCK))
            top0.append(b0)
            top1.append(b1)
            for k in range(i + 1, 8):
                across[i, k] = row[k]
                e[k] = e[k] - m * row[k]
            r0 = r0 - m * b0
            r1 = r1 - m * b1
            pivots = jnp.where(sub == i, row[i], pivots)
        scale = lax.rsqrt(pivots)
        w[lo : lo + 8, 0:BLOCK] = r0 * scale
        w[lo : lo + 8, BLOCK : 2 * BLOCK] = r1 * scale
        q = lo + 8
        while q < BLOCK:
            n = min(32, BLOCK - q)

            def tall(x):
                return jnp.concatenate([x] * (n // 8), axis=0) if n > 8 else x

            g0 = w[q : q + n, 0:BLOCK]
            g1 = w[q : q + n, BLOCK : 2 * BLOCK]
            e = [jnp.broadcast_to(g0[:, lo + k : lo + k + 1], (n, BLOCK)) for k in range(8)]
            for i in range(8):
                m = e[i] * tall(recip[i])
                for k in range(i + 1, 8):
                    e[k] = e[k] - m * tall(across[i, k])
                g0 = g0 - m * tall(top0[i])
                g1 = g1 - m * tall(top1[i])
            w[q : q + n, 0:BLOCK] = g0
            w[q : q + n, BLOCK : 2 * BLOCK] = g1
            q += n


def factor_body(start, blocks, fresh, *refs):
    *a, _, s, inv_ref, w = refs
    lane = lax.axis_index("col")
    ri = lax.broadcasted_iota(jnp.int32, (BLOCK, BLOCK), 0)
    ci = lax.broadcasted_iota(jnp.int32, (BLOCK, BLOCK), 1)
    eye = (ri == ci).astype(F32)
    if fresh:
        for away in range(LEAD):
            at = pl.multiple_of((lane + LEAD - away) % LEAD * BLOCK, BLOCK)
            s[:, pl.ds(at, BLOCK)] = a[away][...]
    else:
        s[...] = a[0][...]

    def step(k, carry):
        at = pl.ds(pl.multiple_of(k * BLOCK, BLOCK), BLOCK)
        w[:, 0:BLOCK] = s[at, at]
        w[:, BLOCK : 2 * BLOCK] = eye
        factor_block(w)
        inverse = jnp.where(ri >= ci, w[:, BLOCK : 2 * BLOCK], 0.0)
        inv_ref[pl.ds(pl.multiple_of((k - start) * BLOCK, BLOCK), BLOCK), :] = inverse
        for kk in range(start, min(start + blocks, LEAD - 1)):

            @pl.when(k == kk)
            def _():
                h = (kk + 1) * BLOCK
                u = mm(inverse, s[kk * BLOCK : h, h:], NN)
                s[kk * BLOCK : h, h:] = u
                for i in range(kk + 1, LEAD):
                    o = (i - kk - 1) * BLOCK
                    s[i * BLOCK : (i + 1) * BLOCK, i * BLOCK :] -= mm(
                        u[:, o : o + BLOCK], u[:, o:], TN
                    )

        return carry

    lax.fori_loop(start, start + blocks, step, 0)


def factor(start, blocks, fresh, a, after):
    return call(
        functools.partial(factor_body, start, blocks, fresh),
        "factor",
        (shape(LEADING, LEADING), shape(blocks * BLOCK, BLOCK)),
        [VMEM] * len(a) + [ANY],
        (VMEM, VMEM),
        [pltpu.VMEM((BLOCK, 2 * BLOCK), F32)],
        flops=20 * 1150 * 10**6,
    )(*a, after)


def solve_body(u, inv_low, inv_high, *refs):
    *a, m_ref, t_ref, work = refs
    nb = len(a)
    rows = a[0].shape[0]
    half = nb // 2
    lane = lax.axis_index("col")
    wide = 2 * BLOCK

    def inverse(k):
        source = inv_low if k < half else inv_high
        return source[(k % half) * BLOCK : (k % half + 1) * BLOCK, :]

    inv = []
    for k in range(0, nb, 2):
        x, y = inverse(k), inverse(k + 1)
        link = u[k * BLOCK : (k + 1) * BLOCK, (k + 1) * BLOCK : (k + 2) * BLOCK]
        low = -mm(mm(y, link, NT), x, NN)
        top = jnp.concatenate([x, jnp.zeros_like(x)], axis=1)
        inv.append(split(jnp.concatenate([top, jnp.concatenate([low, y], axis=1)], axis=0)))
    for away in range(nb):
        at = pl.multiple_of((lane + nb - away) % nb * BLOCK, BLOCK)
        work[:, pl.ds(at, BLOCK)] = a[away][...]
    first = (lax.axis_index("front") * lax.axis_size("row") + lax.axis_index("row")) * rows
    ri = first + lax.broadcasted_iota(jnp.int32, (rows, wide), 0)
    ci = lax.broadcasted_iota(jnp.int32, (rows, wide), 1)
    beyond = []
    for k in range(nb // 2):
        at = slice(k * wide, (k + 1) * wide)
        rest = slice((k + 1) * wide, None)
        m = mm3(split(work[:, at]), inv[k], NT)
        work[:, at] = m
        m_ref[:, at] = jnp.where(ri >= ci + k * wide, m, 0.0)
        if k + 1 < nb // 2:
            beyond.append(split(u[at, rest]))
            work[:, rest] -= mm3(split(m), beyond[k], NN)
    found = None
    for k in reversed(range(nb // 2)):
        at = slice(k * wide, (k + 1) * wide)
        x = work[:, at]
        if found is not None:
            x = x - mm3(found, beyond[k], NT)
        t = mm3(split(x), inv[k], NN)
        t_ref[:, at] = t
        th, tl = split(t)
        if found is None:
            found = (th, tl)
        else:
            found = tuple(jnp.concatenate(z, axis=1) for z in zip((th, tl), found))


def final_body(per_front, per_col, *refs):
    *tables, t, cols, spilt, base, out = refs
    step = pl.program_id(0)
    width = 2 * BLOCK

    @pl.when(step == 0)
    def _():
        out[...] = base[...]
        spill_add(per_front, per_col, 0, *tables, spilt, out)

    tt = split(t[:, pl.ds(pl.multiple_of(step * width, width), width)])
    chunk = 512
    for q in range(0, out.shape[1], chunk):
        other = jnp.concatenate([cols[0, q : q + chunk, :], cols[1, q : q + chunk, :]], axis=1)
        out[:, q : q + chunk] -= mm3(tt, split(other), NT)

    @pl.when(step == pl.num_programs(0) - 1)
    def _():
        top = lax.axis_index("front") * lax.axis_size("row") + lax.axis_index("row")

        @pl.when(top * out.shape[0] < LEADING)
        def _():
            out[...] = jnp.zeros_like(out)

        @pl.when(lax.axis_index("col") * out.shape[1] < LEADING)
        def _():
            out[:, :LEADING] = jnp.zeros((out.shape[0], LEADING), F32)


def from_lanes(parts, lanes):
    return parts[:1] + [
        lax.ppermute(parts[k], "col", [(i, (i + k) % lanes) for i in range(lanes)])
        for k in range(1, lanes)
    ]


def on_device(front_entries, child_updates, off, cnt):
    fronts = lax.axis_size("front")
    rows = lax.axis_size("row")
    cols = lax.axis_size("col")
    own_rows, own_cols = front_entries.shape
    owned = own_rows // BLOCK
    per_front = owned * rows
    per_col = own_cols // BLOCK
    r = lax.axis_index("row")
    c = lax.axis_index("col")
    row_blocks = off.shape[1] // rows
    block = (BLOCK, BLOCK)

    lead = call(
        lead_columns_body, "lead_columns", shape(cols, *block), [SMEM, SMEM, VMEM], VMEM
    )(off, cnt, child_updates)
    lead = lax.all_to_all(lead, "col", split_axis=0, concat_axis=0, tiled=True)
    strips = [front_entries[:, k * BLOCK : (k + 1) * BLOCK] for k in range(LEAD)]
    strip = jnp.where(c == 0, strips[0], 0.0)
    for k in range(1, cols):
        strip = strip + lax.ppermute(strips[k], "col", [(0, k)])
    lead = call(
        functools.partial(lead_rows_body, per_front),
        "lead_rows",
        shape(fronts, 2, *block),
        [SMEM, SMEM, VMEM],
        VMEM,
    )(off, cnt, lead)
    early = lead
    lead = lax.all_to_all(lead, "front", split_axis=0, concat_axis=0, tiled=True)

    table = jax.ShapeDtypeStruct(off.shape, jnp.int32)
    line = jax.ShapeDtypeStruct((off.size,), jnp.int32)
    place, holder, items, pair, sizes = call(
        functools.partial(plan_body, per_col, cols),
        "plan",
        (
            table,
            jax.ShapeDtypeStruct((off.shape[0], off.shape[1] + 1), jnp.int32),
            jax.ShapeDtypeStruct((off.size + 1,), jnp.int32),
            line,
            jax.ShapeDtypeStruct((2,), jnp.int32),
        ),
        [SMEM, SMEM, ANY],
        (SMEM,) * 5,
        [pltpu.SMEM((n,), jnp.int32) for n in (cols, cols * cols, 2)],
    )(off, cnt, early)
    rest = call(
        far_columns_body,
        "far_columns",
        shape(cols, SLOTS, *block),
        [SMEM, ANY],
        ANY,
        [pltpu.SemaphoreType.DMA((off.shape[1],))],
        moved=4 << 20,
    )(place, child_updates)
    planned = rest
    parts = from_lanes([rest[k : k + 1] for k in range(cols)], cols)
    rest = call(
        functools.partial(far_rows_body, per_front),
        "far_rows",
        shape(fronts, 2, SLOTS, *block),
        [SMEM, SMEM] + [VMEM] * cols,
        ANY,
        [pltpu.SemaphoreType.DMA((row_blocks,))],
        moved=8 << 20,
    )(off, cnt, *parts)

    strip = call(
        functools.partial(piece_body, per_front),
        "piece",
        shape(own_rows, BLOCK),
        [SMEM, SMEM, VMEM, VMEM, ANY],
        VMEM,
    )(off, cnt, lead, strip, planned)

    swap = [
        ((i * rows + j) * cols + k, (k * rows + j) * cols + i)
        for i in range(fronts)
        for j in range(rows)
        for k in range(cols)
    ]
    across = lax.ppermute(strip, ("front", "row", "col"), swap)

    piece = jnp.where(lax.axis_index("front") == 0, strip, 0.0)
    for k in range(2, fronts, 2):
        piece = piece + lax.ppermute(strip, "front", [(0, k)])
    odd = lax.ppermute(piece, "front", [(k, k + 1) for k in range(0, fronts, 2)])
    piece = piece + odd
    near = lax.ppermute(piece, "row", [(0, 1), (1, 0)])
    side = lax.ppermute(piece, "row", [(0, 3), (1, 2)])
    far = lax.ppermute(piece, "row", [(0, 2), (1, 3)])
    corner = call(
        gate_body, "gate", shape(2 * own_rows, BLOCK), [VMEM] * 4, VMEM
    )(piece, near, side, far)

    corner = from_lanes([corner] * cols, cols)
    across = lax.all_gather(after(across, near, side, far), ("front", "row"), axis=0)
    across = across.reshape(LEAD, own_cols, BLOCK)
    rest = lax.all_to_all(rest, "front", split_axis=0, concat_axis=0, tiled=True)
    s, inv_low = factor(0, LEAD // 2, True, corner, strip)
    mine = from_lanes([after(strip, inv_low)] * cols, cols)
    s, inv_high = factor(LEAD // 2, LEAD // 2, False, [s], strip)
    m, t = call(
        solve_body,
        "solve",
        (shape(own_rows, LEADING), shape(own_rows, LEADING)),
        [VMEM] * (3 + cols),
        (VMEM, VMEM),
        [pltpu.VMEM((own_rows, LEADING), F32)],
        flops=12 * 1150 * 10**6,
    )(s, inv_low, inv_high, *mine)

    tables = (off, cnt, place, items, pair, sizes)

    def spill(turn):
        spilt = call(
            functools.partial(spill_body, per_col),
            "spill",
            shape(cols, 2, *block),
            [SMEM] * 6 + [VMEM, ANY],
            VMEM,
        )(turn, off, place, items, pair, sizes, rest, inv_high)
        return lax.all_to_all(spilt, "col", split_axis=0, concat_axis=0, tiled=True)

    def another(carry):
        turn, base = carry
        base = call(
            functools.partial(spill_add_body, per_front, per_col),
            "spill_add",
            shape(own_rows, own_cols),
            [SMEM] * 7 + [VMEM, VMEM],
            VMEM,
            input_output_aliases={8: 0},
        )(turn, *tables, spill(turn), base)
        return turn + 1, base

    whole = pl.BlockSpec((own_rows, own_cols), lambda i: (0, 0))
    assembled = pl.pallas_call(
        functools.partial(assemble_body, per_front, per_col),
        name="assemble",
        grid=(fronts // 2,),
        out_shape=shape(own_rows, own_cols),
        in_specs=[SMEM] * 3
        + [pl.BlockSpec((2, 2, SLOTS, *block), lambda i: (i, 0, 0, 0, 0)), whole, ANY],
        out_specs=whole,
        compiler_params=pltpu.CompilerParams(vmem_limit_bytes=48 << 20),
        cost_estimate=pl.CostEstimate(flops=0, bytes_accessed=12 << 20, transcendentals=0),
    )(off, cnt, holder, rest, front_entries, inv_high)
    trailing = pl.pallas_call(
        functools.partial(final_body, per_front, per_col),
        name="final",
        grid=(LEAD // 2,),
        out_shape=shape(own_rows, own_cols),
        in_specs=[SMEM] * 6
        + [
            pl.BlockSpec((own_rows, LEADING), lambda i: (0, 0)),
            pl.BlockSpec((2, own_cols, BLOCK), lambda i: (i, 0, 0)),
            pl.BlockSpec((cols, 2, *block), lambda i: (0, 0, 0, 0)),
            whole,
        ],
        out_specs=whole,
        compiler_params=pltpu.CompilerParams(vmem_limit_bytes=56 << 20),
        cost_estimate=pl.CostEstimate(
            flops=12 * 1150 * 10**6, bytes_accessed=24 << 20, transcendentals=0
        ),
    )(*tables, t, across, spill(jnp.zeros((1,), jnp.int32)), assembled)
    _, trailing = lax.while_loop(
        lambda carry: carry[0][0] < sizes[1], another, (jnp.ones((1,), jnp.int32), trailing)
    )
    return trailing, m


def solution(mesh):
    placed = (P(("front", "row"), "col"), P("front", ("row", "col"), None), P(), P())
    return jax.shard_map(
        on_device,
        mesh=mesh,
        in_specs=placed,
        out_specs=(P(("front", "row"), "col"), P(("front", "row"), None)),
        check_vma=False,
    )
```

```python
import functools

import jax
import jax.numpy as jnp
from jax import lax
from jax.experimental import pallas as pl
from jax.experimental.pallas import tpu as pltpu
from jax.sharding import PartitionSpec as P

BLOCK = 128
LEAD = 8
LEADING = LEAD * BLOCK
SLOTS = 4
HIGHEST = lax.Precision.HIGHEST
NN = (((1,), (0,)), ((), ()))
NT = (((1,), (1,)), ((), ()))
TN = (((0,), (0,)), ((), ()))
F32 = jnp.float32
SMEM = pl.BlockSpec(memory_space=pltpu.SMEM)
VMEM = pl.BlockSpec(memory_space=pltpu.VMEM)
ANY = pl.BlockSpec(memory_space=pl.ANY)


def mm(a, b, dims):
    return lax.dot_general(a, b, dims, precision=HIGHEST, preferred_element_type=F32)


def split(x):
    high = x.astype(jnp.bfloat16)
    low = (x - high.astype(F32)).astype(jnp.bfloat16)
    return high, low


def mm3(a, b, dims):
    ah, al = a
    bh, bl = b
    dot = functools.partial(lax.dot_general, dimension_numbers=dims, preferred_element_type=F32)
    return dot(ah, bh) + (dot(al, bh) + dot(ah, bl))


def call(body, name, out_shape, in_specs, out_specs, scratch=(), flops=0, moved=0, **more):
    return pl.pallas_call(
        body,
        name=name,
        out_shape=out_shape,
        in_specs=in_specs,
        out_specs=out_specs,
        scratch_shapes=list(scratch),
        compiler_params=pltpu.CompilerParams(vmem_limit_bytes=48 << 20),
        cost_estimate=pl.CostEstimate(flops=flops, bytes_accessed=moved, transcendentals=0),
        **more,
    )


def shape(*dims):
    return jax.ShapeDtypeStruct(dims, F32)


def lead_columns_body(off, cnt, child, out):
    g = lax.axis_index("front")
    own = lax.axis_index("row") * lax.axis_size("col") + lax.axis_index("col")
    out[...] = jnp.zeros_like(out)
    live = cnt[g]
    for b in range(off.shape[1]):
        o = off[g, b]

        @pl.when((o < LEAD) & (b < live) & (own < live))
        def _():
            out[o] = child[0, :, b * BLOCK : (b + 1) * BLOCK]


def lead_rows_body(per_front, off, cnt, got, out):
    g = lax.axis_index("front")
    r = lax.axis_index("row")
    rows = got.shape[0]
    out[...] = jnp.zeros_like(out)
    for j in range(rows):
        f = off[g, r * rows + j] // per_front
        rank = jnp.int32(0)
        for i in range(j):
            rank += (off[g, r * rows + i] // per_front == f).astype(jnp.int32)
        out[f, rank] = got[j]


def piece_body(per_front, off, cnt, got, base, _, out):
    r = lax.axis_index("row")
    own = lax.axis_index("front")
    rows = off.shape[1] // lax.axis_size("row")
    owned = out.shape[0] // BLOCK
    out[...] = base[...]

    def child(g, carry):
        rank = jnp.int32(0)
        for j in range(rows):
            a = r * rows + j
            o = off[g, a]
            hit = o // per_front == own
            at = pl.ds(pl.multiple_of((o % owned) * BLOCK, BLOCK), BLOCK)
            here = rank

            @pl.when(hit & (a < cnt[g]))
            def _():
                out[at, :] += got[g, here]

            rank += hit.astype(jnp.int32)
        return carry

    lax.fori_loop(0, got.shape[0], child, 0)


def plan_body(
    per_col, lanes, off, cnt, _, place, holder, items, pair, sizes, taken, pairs, swap
):
    children, blocks = off.shape
    for i in range(lanes * lanes):
        pairs[i] = 0
    sizes[0] = 0
    sizes[1] = 0

    def child(g, carry):
        for m in range(lanes):
            taken[m] = 0
        for b in range(blocks):
            holder[g, b] = -1
        first = sizes[0]
        live = cnt[g]

        def own_lane(b, n):
            o = off[g, b]
            c = o // per_col
            k = taken[c]
            use = (o >= LEAD) & (b < live)
            fits = use & (k < SLOTS)
            at = c * SLOTS + k
            place[g, b] = jnp.where(fits, at, -1)
            holder[g, jnp.where(fits, at, blocks)] = b
            taken[c] = k + fits.astype(jnp.int32)
            items[n] = g * blocks + b
            return n + (use & (k >= SLOTS)).astype(jnp.int32)

        last = lax.fori_loop(0, blocks, own_lane, first, unroll=4)
        sizes[0] = last

        def other_lane(n, carry):
            b = items[n] % blocks
            c = off[g, b] // per_col
            best = jnp.int32(1 << 20)
            lane = jnp.int32(0)
            for m in range(lanes):
                score = jnp.where(taken[m] < SLOTS, pairs[m * lanes + c], 1 << 20)
                lane = jnp.where(score < best, m, lane)
                best = jnp.minimum(score, best)

            def put(n, b, lane, c):
                place[g, b] = lane * SLOTS + taken[lane]
                pair[n] = pairs[lane * lanes + c]
                taken[lane] += 1
                pairs[lane * lanes + c] += 1
                sizes[1] = jnp.maximum(sizes[1], pairs[lane * lanes + c])

            swap[0] = -1
            swap[1] = -1

            @pl.when(best > 0)
            def _():
                via = jnp.int32(-1)
                to = jnp.int32(-1)
                for m in range(lanes):
                    for v in range(lanes):
                        if v != m:
                            own = holder[g, v * SLOTS]
                            ok = (via < 0) & (own >= 0) & (v != c) & (m != c)
                            ok &= (taken[m] < SLOTS) & (pairs[m * lanes + v] == 0)
                            ok &= pairs[v * lanes + c] == 0
                            via = jnp.where(ok, v, via)
                            to = jnp.where(ok, m, to)
                swap[0] = via
                swap[1] = to

            via = swap[0]
            to = swap[1]

            @pl.when(via < 0)
            def _():
                put(n, b, lane, c)

            @pl.when(via >= 0)
            def _():
                own = holder[g, via * SLOTS]
                holder[g, via * SLOTS] = -1
                more = sizes[0]
                sizes[0] = more + 1
                items[more] = g * blocks + own
                put(more, own, to, via)
                place[g, b] = via * SLOTS
                pair[n] = 0
                pairs[via * lanes + c] = 1
                sizes[1] = jnp.maximum(sizes[1], 1)

            return carry

        lax.fori_loop(first, last, other_lane, 0)
        return carry

    lax.fori_loop(0, children, child, 0)


def far_columns_body(place, child, out, sems):
    g = lax.axis_index("front")
    c = lax.axis_index("col")
    lanes = out.shape[0]
    copies = []
    for b in range(place.shape[1]):
        p = place[g, b]
        to = jnp.maximum(p, 0)
        copy = pltpu.make_async_copy(
            child.at[0, :, pl.ds(b * BLOCK, BLOCK)],
            out.at[(to // SLOTS + lanes - c) % lanes, to % SLOTS],
            sems.at[b],
        )
        copies.append((p >= 0, copy))

        @pl.when(p >= 0)
        def _():
            copy.start()

    for use, copy in copies:

        @pl.when(use)
        def _():
            copy.wait()


def far_rows_body(per_front, off, cnt, *refs):
    *got, out, sems = refs
    g = lax.axis_index("front")
    r = lax.axis_index("row")
    c = lax.axis_index("col")
    rows = len(got)
    copies = []
    for away in range(rows):
        j = (c + rows - away) % rows
        a = r * rows + j
        o = off[g, a]
        f = o // per_front
        rank = jnp.int32(0)
        for i in range(rows):
            rank += ((off[g, r * rows + i] // per_front == f) & (i < j)).astype(jnp.int32)
        use = (o >= LEAD) & (a < cnt[g])
        copy = pltpu.make_async_copy(
            got[away].at[0], out.at[f, jnp.minimum(rank, 1)], sems.at[away]
        )
        copies.append((use, copy))

        @pl.when(use)
        def _():
            copy.start()

    for use, copy in copies:

        @pl.when(use)
        def _():
            copy.wait()


def spill_body(per_col, turn, off, place, items, pair, sizes, got, _, out):
    c = lax.axis_index("col")
    out[...] = jnp.zeros_like(out)
    blocks = off.shape[1]

    def item(n, carry):
        g = items[n] // blocks
        b = items[n] % blocks
        p = place[g, b]

        @pl.when((pair[n] == turn[0]) & (p // SLOTS == c))
        def _():
            out[off[g, b] // per_col] = got[g, :, p % SLOTS]

        return carry

    lax.fori_loop(0, sizes[0], item, 0)


def each_row(per_front, g, off, cnt, add):
    f = lax.axis_index("front")
    r = lax.axis_index("row")
    rows = off.shape[1] // lax.axis_size("row")
    owned = per_front // lax.axis_size("row")
    rank = jnp.int32(0)
    for j in range(rows):
        a = r * rows + j
        o = off[g, a]
        hit = o // per_front == f
        row = pl.ds(pl.multiple_of((o % owned) * BLOCK, BLOCK), BLOCK)
        here = rank

        @pl.when(hit & (a < cnt[g]) & (o >= LEAD))
        def _():
            add(row, here)

        rank += hit.astype(jnp.int32)


def own_column(per_col, p):
    return pl.ds(pl.multiple_of((p % per_col) * BLOCK, BLOCK), BLOCK)


def spill_add(per_front, per_col, turn, off, cnt, place, items, pair, sizes, spilt, out):
    c = lax.axis_index("col")
    blocks = off.shape[1]

    def item(n, carry):
        g = items[n] // blocks
        b = items[n] % blocks
        p = off[g, b]
        lane = jnp.maximum(place[g, b], 0) // SLOTS

        @pl.when((pair[n] == turn) & (p // per_col == c))
        def _():
            def add(row, rank):
                out[row, own_column(per_col, p)] += spilt[lane, rank]

            each_row(per_front, g, off, cnt, add)

        return carry

    lax.fori_loop(0, sizes[0], item, 0)


def spill_add_body(per_front, per_col, turn, off, cnt, place, items, pair, sizes, spilt, base, out):
    out[...] = base[...]
    spill_add(per_front, per_col, turn[0], off, cnt, place, items, pair, sizes, spilt, out)


def assemble_body(per_front, per_col, off, cnt, holder, got, base, _, out):
    c = lax.axis_index("col")
    step = pl.program_id(0)

    @pl.when(step == 0)
    def _():
        out[...] = base[...]

    for half in range(got.shape[0]):
        g = got.shape[0] * step + half

        def add(row, rank):
            for k in range(SLOTS):
                b = holder[g, c * SLOTS + k]

                @pl.when(b >= 0)
                def _():
                    at = own_column(per_col, off[g, jnp.maximum(b, 0)])
                    out[row, at] += got[half, rank, k]

        each_row(per_front, g, off, cnt, add)


def gate_body(piece, near, side, far, corner):
    r = lax.axis_index("row")
    half = piece.shape[0]
    for k, (upper, lower) in enumerate(((piece, near), (near, piece), (far, side), (side, far))):

        @pl.when(r == k)
        def _():
            corner[:half] = upper[...]
            corner[half:] = lower[...]


def after_body(x, *refs):
    refs[-1][...] = x[...]


def after(x, *others):
    return call(
        after_body, "after", shape(*x.shape), [VMEM] + [ANY] * len(others), VMEM, moved=8 * x.size
    )(x, *others)


def factor_block(w):
    sub = lax.broadcasted_iota(jnp.int32, (8, BLOCK), 0)
    for lo in range(0, BLOCK, 8):
        r0 = w[lo : lo + 8, 0:BLOCK]
        r1 = w[lo : lo + 8, BLOCK : 2 * BLOCK]
        e = [jnp.broadcast_to(r0[:, lo + k : lo + k + 1], (8, BLOCK)) for k in range(8)]
        recip, across, top0, top1 = [], {}, [], []
        pivots = jnp.ones((8, BLOCK), F32)
        for i in range(8):
            row = {k: jnp.broadcast_to(e[k][i : i + 1, :], (8, BLOCK)) for k in range(i, 8)}
            inv = 1.0 / row[i]
            recip.append(inv)
            m = jnp.where(sub > i, e[i] * inv, 0.0)
            b0 = jnp.broadcast_to(r0[i : i + 1, :], (8, BLOCK))
            b1 = jnp.broadcast_to(r1[i : i + 1, :], (8, BLOCK))
            top0.append(b0)
            top1.append(b1)
            for k in range(i + 1, 8):
                across[i, k] = row[k]
                e[k] = e[k] - m * row[k]
            r0 = r0 - m * b0
            r1 = r1 - m * b1
            pivots = jnp.where(sub == i, row[i], pivots)
        scale = lax.rsqrt(pivots)
        w[lo : lo + 8, 0:BLOCK] = r0 * scale
        w[lo : lo + 8, BLOCK : 2 * BLOCK] = r1 * scale
        q = lo + 8
        while q < BLOCK:
            n = min(32, BLOCK - q)

            def tall(x):
                return jnp.concatenate([x] * (n // 8), axis=0) if n > 8 else x

            g0 = w[q : q + n, 0:BLOCK]
            g1 = w[q : q + n, BLOCK : 2 * BLOCK]
            e = [jnp.broadcast_to(g0[:, lo + k : lo + k + 1], (n, BLOCK)) for k in range(8)]
            for i in range(8):
                m = e[i] * tall(recip[i])
                for k in range(i + 1, 8):
                    e[k] = e[k] - m * tall(across[i, k])
                g0 = g0 - m * tall(top0[i])
                g1 = g1 - m * tall(top1[i])
            w[q : q + n, 0:BLOCK] = g0
            w[q : q + n, BLOCK : 2 * BLOCK] = g1
            q += n


def factor_body(start, blocks, fresh, a, _, s, inv_ref, w):
    ri = lax.broadcasted_iota(jnp.int32, (BLOCK, BLOCK), 0)
    ci = lax.broadcasted_iota(jnp.int32, (BLOCK, BLOCK), 1)
    eye = (ri == ci).astype(F32)
    if fresh:
        for c in range(LEAD):
            s[:, c * BLOCK : (c + 1) * BLOCK] = a[c]
    else:
        s[...] = a[...]

    def step(k, carry):
        at = pl.ds(pl.multiple_of(k * BLOCK, BLOCK), BLOCK)
        w[:, 0:BLOCK] = s[at, at]
        w[:, BLOCK : 2 * BLOCK] = eye
        factor_block(w)
        inverse = jnp.where(ri >= ci, w[:, BLOCK : 2 * BLOCK], 0.0)
        inv_ref[pl.ds(pl.multiple_of((k - start) * BLOCK, BLOCK), BLOCK), :] = inverse
        for kk in range(start, min(start + blocks, LEAD - 1)):

            @pl.when(k == kk)
            def _():
                h = (kk + 1) * BLOCK
                u = mm(inverse, s[kk * BLOCK : h, h:], NN)
                s[kk * BLOCK : h, h:] = u
                for i in range(kk + 1, LEAD):
                    o = (i - kk - 1) * BLOCK
                    s[i * BLOCK : (i + 1) * BLOCK, i * BLOCK :] -= mm(
                        u[:, o : o + BLOCK], u[:, o:], TN
                    )

        return carry

    lax.fori_loop(start, start + blocks, step, 0)


def factor(start, blocks, fresh, a, after):
    return call(
        functools.partial(factor_body, start, blocks, fresh),
        "factor",
        (shape(LEADING, LEADING), shape(blocks * BLOCK, BLOCK)),
        [VMEM, ANY],
        (VMEM, VMEM),
        [pltpu.VMEM((BLOCK, 2 * BLOCK), F32)],
        flops=20 * 1150 * 10**6,
    )(a, after)


def solve_body(u, inv_low, inv_high, *refs):
    *a, m_ref, t_ref, work = refs
    nb = len(a)
    rows = a[0].shape[0]
    half = nb // 2
    lane = lax.axis_index("col")
    wide = 2 * BLOCK

    def inverse(k):
        source = inv_low if k < half else inv_high
        return source[(k % half) * BLOCK : (k % half + 1) * BLOCK, :]

    inv = []
    for k in range(0, nb, 2):
        x, y = inverse(k), inverse(k + 1)
        link = u[k * BLOCK : (k + 1) * BLOCK, (k + 1) * BLOCK : (k + 2) * BLOCK]
        low = -mm(mm(y, link, NT), x, NN)
        top = jnp.concatenate([x, jnp.zeros_like(x)], axis=1)
        inv.append(split(jnp.concatenate([top, jnp.concatenate([low, y], axis=1)], axis=0)))
    for away in range(nb):
        at = pl.multiple_of((lane + nb - away) % nb * BLOCK, BLOCK)
        work[:, pl.ds(at, BLOCK)] = a[away][...]
    first = (lax.axis_index("front") * lax.axis_size("row") + lax.axis_index("row")) * rows
    ri = first + lax.broadcasted_iota(jnp.int32, (rows, wide), 0)
    ci = lax.broadcasted_iota(jnp.int32, (rows, wide), 1)
    beyond = []
    for k in range(nb // 2):
        at = slice(k * wide, (k + 1) * wide)
        rest = slice((k + 1) * wide, None)
        m = mm3(split(work[:, at]), inv[k], NT)
        work[:, at] = m
        m_ref[:, at] = jnp.where(ri >= ci + k * wide, m, 0.0)
        if k + 1 < nb // 2:
            beyond.append(split(u[at, rest]))
            work[:, rest] -= mm3(split(m), beyond[k], NN)
    found = None
    for k in reversed(range(nb // 2)):
        at = slice(k * wide, (k + 1) * wide)
        x = work[:, at]
        if found is not None:
            x = x - mm3(found, beyond[k], NT)
        t = mm3(split(x), inv[k], NN)
        t_ref[:, at] = t
        th, tl = split(t)
        if found is None:
            found = (th, tl)
        else:
            found = tuple(jnp.concatenate(z, axis=1) for z in zip((th, tl), found))


def final_body(per_front, per_col, *refs):
    *tables, t, cols, spilt, base, out = refs
    step = pl.program_id(0)
    width = 2 * BLOCK

    @pl.when(step == 0)
    def _():
        out[...] = base[...]
        spill_add(per_front, per_col, 0, *tables, spilt, out)

    tt = split(t[:, pl.ds(pl.multiple_of(step * width, width), width)])
    chunk = 512
    for q in range(0, out.shape[1], chunk):
        other = jnp.concatenate([cols[0, q : q + chunk, :], cols[1, q : q + chunk, :]], axis=1)
        out[:, q : q + chunk] -= mm3(tt, split(other), NT)

    @pl.when(step == pl.num_programs(0) - 1)
    def _():
        top = lax.axis_index("front") * lax.axis_size("row") + lax.axis_index("row")

        @pl.when(top * out.shape[0] < LEADING)
        def _():
            out[...] = jnp.zeros_like(out)

        @pl.when(lax.axis_index("col") * out.shape[1] < LEADING)
        def _():
            out[:, :LEADING] = jnp.zeros((out.shape[0], LEADING), F32)


def from_lanes(parts, lanes):
    return parts[:1] + [
        lax.ppermute(parts[k], "col", [(i, (i + k) % lanes) for i in range(lanes)])
        for k in range(1, lanes)
    ]


def on_device(front_entries, child_updates, off, cnt):
    fronts = lax.axis_size("front")
    rows = lax.axis_size("row")
    cols = lax.axis_size("col")
    own_rows, own_cols = front_entries.shape
    owned = own_rows // BLOCK
    per_front = owned * rows
    per_col = own_cols // BLOCK
    r = lax.axis_index("row")
    c = lax.axis_index("col")
    row_blocks = off.shape[1] // rows
    block = (BLOCK, BLOCK)

    lead = call(
        lead_columns_body, "lead_columns", shape(cols, *block), [SMEM, SMEM, VMEM], VMEM
    )(off, cnt, child_updates)
    lead = lax.all_to_all(lead, "col", split_axis=0, concat_axis=0, tiled=True)
    strips = [front_entries[:, k * BLOCK : (k + 1) * BLOCK] for k in range(LEAD)]
    strip = jnp.where(c == 0, strips[0], 0.0)
    for k in range(1, cols):
        strip = strip + lax.ppermute(strips[k], "col", [(0, k)])
    lead = call(
        functools.partial(lead_rows_body, per_front),
        "lead_rows",
        shape(fronts, 2, *block),
        [SMEM, SMEM, VMEM],
        VMEM,
    )(off, cnt, lead)
    early = lead
    lead = lax.all_to_all(lead, "front", split_axis=0, concat_axis=0, tiled=True)

    table = jax.ShapeDtypeStruct(off.shape, jnp.int32)
    line = jax.ShapeDtypeStruct((off.size,), jnp.int32)
    place, holder, items, pair, sizes = call(
        functools.partial(plan_body, per_col, cols),
        "plan",
        (
            table,
            jax.ShapeDtypeStruct((off.shape[0], off.shape[1] + 1), jnp.int32),
            jax.ShapeDtypeStruct((off.size + 1,), jnp.int32),
            line,
            jax.ShapeDtypeStruct((2,), jnp.int32),
        ),
        [SMEM, SMEM, ANY],
        (SMEM,) * 5,
        [pltpu.SMEM((n,), jnp.int32) for n in (cols, cols * cols, 2)],
    )(off, cnt, early)
    rest = call(
        far_columns_body,
        "far_columns",
        shape(cols, SLOTS, *block),
        [SMEM, ANY],
        ANY,
        [pltpu.SemaphoreType.DMA((off.shape[1],))],
        moved=4 << 20,
    )(place, child_updates)
    planned = rest
    parts = from_lanes([rest[k : k + 1] for k in range(cols)], cols)
    rest = call(
        functools.partial(far_rows_body, per_front),
        "far_rows",
        shape(fronts, 2, SLOTS, *block),
        [SMEM, SMEM] + [VMEM] * cols,
        ANY,
        [pltpu.SemaphoreType.DMA((row_blocks,))],
        moved=8 << 20,
    )(off, cnt, *parts)

    strip = call(
        functools.partial(piece_body, per_front),
        "piece",
        shape(own_rows, BLOCK),
        [SMEM, SMEM, VMEM, VMEM, ANY],
        VMEM,
    )(off, cnt, lead, strip, planned)

    piece = jnp.where(lax.axis_index("front") == 0, strip, 0.0)
    for k in range(2, fronts, 2):
        piece = piece + lax.ppermute(strip, "front", [(0, k)])
    odd = lax.ppermute(piece, "front", [(k, k + 1) for k in range(0, fronts, 2)])
    piece = after(piece + odd, *parts[1:])
    near = lax.ppermute(piece, "row", [(0, 1), (1, 0)])
    side = lax.ppermute(piece, "row", [(0, 3), (1, 2)])
    far = lax.ppermute(piece, "row", [(0, 2), (1, 3)])
    corner = call(
        gate_body, "gate", shape(2 * own_rows, BLOCK), [VMEM] * 4, VMEM
    )(piece, near, side, far)

    swap = [
        ((i * rows + j) * cols + k, (k * rows + j) * cols + i)
        for i in range(fronts)
        for j in range(rows)
        for k in range(cols)
    ]
    across = after(lax.ppermute(strip, ("front", "row", "col"), swap), corner)
    corner = lax.all_gather(corner, "col", axis=0)
    across = lax.all_gather(across, ("front", "row"), axis=0)
    across = across.reshape(LEAD, own_cols, BLOCK)
    rest = lax.all_to_all(rest, "front", split_axis=0, concat_axis=0, tiled=True)
    s, inv_low = factor(0, LEAD // 2, True, corner, strip)
    mine = from_lanes([after(strip, inv_low)] * cols, cols)
    s, inv_high = factor(LEAD // 2, LEAD // 2, False, s, strip)
    m, t = call(
        solve_body,
        "solve",
        (shape(own_rows, LEADING), shape(own_rows, LEADING)),
        [VMEM] * (3 + cols),
        (VMEM, VMEM),
        [pltpu.VMEM((own_rows, LEADING), F32)],
        flops=12 * 1150 * 10**6,
    )(s, inv_low, inv_high, *mine)

    tables = (off, cnt, place, items, pair, sizes)

    def spill(turn):
        spilt = call(
            functools.partial(spill_body, per_col),
            "spill",
            shape(cols, 2, *block),
            [SMEM] * 6 + [VMEM, ANY],
            VMEM,
        )(turn, off, place, items, pair, sizes, rest, inv_high)
        return lax.all_to_all(spilt, "col", split_axis=0, concat_axis=0, tiled=True)

    def another(carry):
        turn, base = carry
        base = call(
            functools.partial(spill_add_body, per_front, per_col),
            "spill_add",
            shape(own_rows, own_cols),
            [SMEM] * 7 + [VMEM, VMEM],
            VMEM,
            input_output_aliases={8: 0},
        )(turn, *tables, spill(turn), base)
        return turn + 1, base

    whole = pl.BlockSpec((own_rows, own_cols), lambda i: (0, 0))
    assembled = pl.pallas_call(
        functools.partial(assemble_body, per_front, per_col),
        name="assemble",
        grid=(fronts // 2,),
        out_shape=shape(own_rows, own_cols),
        in_specs=[SMEM] * 3
        + [pl.BlockSpec((2, 2, SLOTS, *block), lambda i: (i, 0, 0, 0, 0)), whole, ANY],
        out_specs=whole,
        compiler_params=pltpu.CompilerParams(vmem_limit_bytes=48 << 20),
        cost_estimate=pl.CostEstimate(flops=0, bytes_accessed=12 << 20, transcendentals=0),
    )(off, cnt, holder, rest, front_entries, inv_high)
    trailing = pl.pallas_call(
        functools.partial(final_body, per_front, per_col),
        name="final",
        grid=(LEAD // 2,),
        out_shape=shape(own_rows, own_cols),
        in_specs=[SMEM] * 6
        + [
            pl.BlockSpec((own_rows, LEADING), lambda i: (0, 0)),
            pl.BlockSpec((2, own_cols, BLOCK), lambda i: (i, 0, 0)),
            pl.BlockSpec((cols, 2, *block), lambda i: (0, 0, 0, 0)),
            whole,
        ],
        out_specs=whole,
        compiler_params=pltpu.CompilerParams(vmem_limit_bytes=56 << 20),
        cost_estimate=pl.CostEstimate(
            flops=12 * 1150 * 10**6, bytes_accessed=24 << 20, transcendentals=0
        ),
    )(*tables, t, across, spill(jnp.zeros((1,), jnp.int32)), assembled)
    _, trailing = lax.while_loop(
        lambda carry: carry[0][0] < sizes[1], another, (jnp.ones((1,), jnp.int32), trailing)
    )
    return trailing, m


def solution(mesh):
    placed = (P(("front", "row"), "col"), P("front", ("row", "col"), None), P(), P())
    return jax.shard_map(
        on_device,
        mesh=mesh,
        in_specs=placed,
        out_specs=(P(("front", "row"), "col"), P(("front", "row"), None)),
        check_vma=False,
    )
```
